256 devices in a mesh: dp: 16 (over z, y_hi), seq: 8 (over x, core), mp: 2 (over y_lo).
Axes of the slice: x: 4, y: 4 (y_hi: 2, y_lo: 2; y = y_hi * 2 + y_lo), z: 8, core: 2. Of those that a mesh axis runs over, the one named last changes fastest.
Arguments:
- query: bfloat16 [16, 2048, 4096], P('dp', 'seq', 'mp'), may hold values from -60 to 60
- latents: bfloat16 [16, 48, 64, 1280], P('dp', ('seq', 'mp')), may hold values from -6 to 6
- image_slot: int32 [16, 16], P('dp'), may hold values from 0 to 47, as said below
- block_image: int32 [16, 64], P('dp'), may hold values from 0 to 15, as said below
- key_weight: bfloat16 [1280, 2, 2048], P(None, 'mp', 'seq'), may hold values from -0.15625 to 0.15625
- value_weight: bfloat16 [1280, 2, 2048], P(None, 'mp', 'seq'), may hold values from -0.15625 to 0.15625
- gate: float32 [32], P('mp'), may hold values from 0.2 to 2
- cotangent: bfloat16 [16, 2048, 4096], P('dp', 'seq', 'mp'), may hold values from -6 to 6
Outputs:
- attended: bfloat16 [16, 2048, 4096], P('dp', 'seq', 'mp')
- query_grad: bfloat16 [16, 2048, 4096], P('dp', 'seq', 'mp')
- key_grad: float32 [1280, 2, 2048], P('dp', 'mp', 'seq')
- value_grad: float32 [1280, 2, 2048], P('dp', 'mp', 'seq')
The draws below stay inside these ranges and needn't reach their ends.
Inputs may be any that keep to these rules, and one draw needn't show every extreme that they name: `image_slot`: within a document the images sit in distinct slots; each vision device (slots k * 3 to (k + 1) * 3 - 1) holds at most 3 of them, and some device holds exactly 3. `block_image`: within a document it never falls from one text block to the next, starts at 0, and names every one of the 16 images.
All inputs are finite; a program needn't handle non-finite values.
Results may differ from the reference program's by a relative error of at most 0.02.
The reference program's roundings to bfloat16 on the way count: a program that leaves them out, or rounds other values in their place, can miss the bound.
Values may be sent and summed in bfloat16 or wider, within the bound.
No kernel may reach another device: no remote copies, remote signals or barrier semaphores. Data moves between devices by JAX's collectives and lax.ppermute only.
A program may use at most 128 MiB of HBM per device.

```python
import math
import jax
import jax.numpy as jnp
from jax import lax

KV = 1280
HEADS = 32
HD = 128
LAT = 64
IMAGES = 16
SLOTS = 3
TEXT_BLOCK = 32
DOCS = 16
SEQ_LEN = 2048
BLOCKS = 64
HH = 4096
SLOT_ALL = 48
N_SEQ = 8
N_MP = 2


def draw_query(key, part):
    key = jax.random.fold_in(key, 5)
    first = jax.random.fold_in(key, 0)
    base = jnp.clip(jax.random.normal(first, (DOCS, SEQ_LEN, HH), jnp.float32), -6.0, 6.0)
    return base.astype(jnp.bfloat16)


def draw_image_slot(key, part):
    key = jax.random.fold_in(key, 11)
    holders = N_SEQ * N_MP

    def one_doc(doc_key):
        first, second, third = jax.random.split(doc_key, 3)
        busiest = jax.random.randint(first, (), 0, holders)
        order = jax.random.permutation(second, IMAGES)
        others = jax.random.permutation(third, (holders - 1) * SLOTS)[:IMAGES - SLOTS]
        others = jnp.where(others >= busiest * SLOTS, others + SLOTS, others)
        chosen = jnp.concatenate([busiest * SLOTS + jnp.arange(SLOTS, dtype=jnp.int32), others.astype(jnp.int32)])
        return jnp.zeros((IMAGES,), jnp.int32).at[order].set(chosen.astype(jnp.int32))
    return jax.vmap(one_doc)(jax.random.split(key, DOCS))


def draw_block_image(key, part):
    key = jax.random.fold_in(key, 12)

    def one_doc(doc_key):
        starts = jax.random.permutation(doc_key, BLOCKS - 1)[:IMAGES - 1] + 1
        places = jnp.arange(BLOCKS, dtype=jnp.int32)
        return jnp.sum((places[:, None] >= starts[None, :]).astype(jnp.int32), axis=1).astype(jnp.int32)
    return jax.vmap(one_doc)(jax.random.split(key, DOCS))


def strengthened(values, rng, source, target, shards_of, factor):
    owner, partner = [(jnp.arange(values.shape[axis_at]) // (values.shape[axis_at] // shards_of)).reshape([-1 if axis == axis_at else 1 for axis in range(values.ndim)]) for axis_at in (source, target)]
    chosen = jax.random.permutation(rng, shards_of)[partner]
    strong = (owner == chosen) | (owner == (partner + shards_of // 2) % shards_of)
    return jnp.where(strong, factor * values, values)


def block_levels(rng, dims, cuts, smallest, largest):
    loudness, own = 1.0, jax.random.fold_in(rng, 6)
    for position, shards_of in cuts:
        steps = jnp.exp(jax.random.uniform(jax.random.fold_in(own, position), (shards_of,), jnp.float32, smallest / len(cuts), largest / len(cuts)))
        loudness = loudness * jnp.repeat(steps, dims[position] // shards_of).reshape([-1 if axis == position else 1 for axis in range(len(dims))])
    return loudness


def scatter_about(own_key, shape, width, reach, cuts=(), kind=jnp.bfloat16):
    result = width * jax.random.normal(own_key, shape, jnp.float32)
    if cuts:
        result = result * block_levels(own_key, shape, cuts, -0.22, 0.18)
    return jnp.clip(result, -reach, reach).astype(kind)


def gaussian_with(rng, extent, width, bound, cuts, heavy, kind=jnp.bfloat16):
    result = width * jax.random.normal(rng, extent, jnp.float32)
    if cuts:
        result = result * block_levels(rng, extent, cuts, -0.22, 0.18)
    return jnp.clip(strengthened(result, jax.random.fold_in(rng, 3), *heavy), -bound, bound).astype(kind)


def setup_inputs(seed: int = 0) -> dict:
    seeds = jax.random.split(jax.random.key(seed), 9)
    query = draw_query(jax.random.fold_in(seeds[8], 71), 0)
    latents = gaussian_with(seeds[1], (DOCS, SLOT_ALL, LAT, KV), 1.0, 6.0, ((0, 16), (1, 16)), (0, 3, 16, 2.0))
    image_slot = draw_image_slot(jax.random.fold_in(seeds[8], 71), 0)
    block_image = draw_block_image(jax.random.fold_in(seeds[8], 71), 0)
    key_weight = scatter_about(seeds[4], (KV, N_MP, HH // N_MP), KV ** -0.5, 0.15625, ((1, 2), (2, 8)))
    value_weight = scatter_about(seeds[5], (KV, N_MP, HH // N_MP), KV ** -0.5, 0.15625, ((1, 2), (2, 8)))
    gate = jnp.clip(0.2 + 1.8 * jax.random.uniform(seeds[6], (HEADS,), jnp.float32) ** block_levels(seeds[6], (HEADS,), ((0, 2),), -0.2, 0.2), 0.2, 2.0)
    cotangent = scatter_about(seeds[7], (DOCS, SEQ_LEN, HH), 1.0, 6.0, ((0, 16), (1, 8), (2, 2)))
    return {"query": query, "latents": latents, "image_slot": image_slot, "block_image": block_image, "key_weight": key_weight, "value_weight": value_weight, "gate": gate, "cotangent": cotangent}


def reference(query, latents, image_slot, block_image, key_weight, value_weight, gate, cotangent):
    key_proj = key_weight.reshape(KV, HH)
    value_proj = value_weight.reshape(KV, HH)
    scale = 1.0 / math.sqrt(HD)
    gain = jnp.tanh(gate.astype(jnp.float32))[None, None, :, None]

    def one_doc(carry, inputs):
        text_query, slot_latents, slot_of, blocks_of, text_grad = inputs
        flat = jnp.take(slot_latents, slot_of, axis=0).reshape(IMAGES * LAT, KV)
        keys = jnp.dot(flat, key_proj, preferred_element_type=jnp.float32).astype(jnp.bfloat16)
        values = jnp.dot(flat, value_proj, preferred_element_type=jnp.float32).astype(jnp.bfloat16)
        keys = keys.reshape(IMAGES, LAT, HEADS, HD)
        values = values.reshape(IMAGES, LAT, HEADS, HD)
        key_blocks = jnp.take(keys, blocks_of, axis=0).astype(jnp.float32)
        value_blocks = jnp.take(values, blocks_of, axis=0).astype(jnp.float32)
        queries = text_query.reshape(BLOCKS, TEXT_BLOCK, HEADS, HD).astype(jnp.float32)
        score = jnp.einsum('bthd,blhd->bhtl', queries, key_blocks) * scale
        prob = jax.nn.softmax(score, axis=-1)
        prob_low = prob.astype(jnp.bfloat16).astype(jnp.float32)
        mixed = jnp.einsum('bhtl,blhd->bthd', prob_low, value_blocks)
        attended = (mixed * gain).astype(jnp.bfloat16).reshape(SEQ_LEN, HH)
        gated = (text_grad.reshape(BLOCKS, TEXT_BLOCK, HEADS, HD).astype(jnp.float32) * gain).astype(jnp.bfloat16).astype(jnp.float32)
        prob_grad = jnp.einsum('bthd,blhd->bhtl', gated, value_blocks)
        delta = lax.optimization_barrier(jnp.sum(prob_grad * prob, axis=-1, keepdims=True))
        score_grad = (prob * (prob_grad - delta) * scale).astype(jnp.bfloat16).astype(jnp.float32)
        query_grad = jnp.einsum('bhtl,blhd->bthd', score_grad, key_blocks).astype(jnp.bfloat16).reshape(SEQ_LEN, HH)
        key_term = jnp.einsum('bhtl,bthd->blhd', score_grad, queries).astype(jnp.bfloat16).astype(jnp.float32)
        value_term = jnp.einsum('bhtl,bthd->blhd', prob_low, gated).astype(jnp.bfloat16).astype(jnp.float32)
        onehot = (blocks_of[None, :] == jnp.arange(IMAGES, dtype=jnp.int32)[:, None]).astype(jnp.float32)
        key_image = jnp.einsum('ib,blhd->ilhd', onehot, key_term).astype(jnp.bfloat16).reshape(IMAGES * LAT, HH)
        value_image = jnp.einsum('ib,blhd->ilhd', onehot, value_term).astype(jnp.bfloat16).reshape(IMAGES * LAT, HH)
        key_part = jnp.dot(flat.T, key_image, preferred_element_type=jnp.float32)
        value_part = jnp.dot(flat.T, value_image, preferred_element_type=jnp.float32)
        return ((carry[0] + key_part, carry[1] + value_part), (attended, query_grad))
    start = (jnp.zeros((KV, HH), jnp.float32), jnp.zeros((KV, HH), jnp.float32))
    totals, outputs = lax.scan(one_doc, start, (query, latents, image_slot, block_image, cotangent))
    key_grad = totals[0].reshape(KV, N_MP, HH // N_MP)
    value_grad = totals[1].reshape(KV, N_MP, HH // N_MP)
    return (outputs[0], outputs[1], key_grad, value_grad)
```

```python
import math

import jax
import jax.numpy as jnp
from jax import lax
from jax.experimental import pallas as pl
from jax.experimental.pallas import tpu as pltpu
from jax.sharding import PartitionSpec as P

F32, BF16 = jnp.float32, jnp.bfloat16
IMAGES, LAT, HD, TB, UNROLL = 16, 64, 128, 32, 8
PIECES = 8
ROWS = LAT // PIECES
VMEM = pl.BlockSpec(memory_space=pltpu.VMEM)
SMEM = pl.BlockSpec(memory_space=pltpu.SMEM)


def dot(a, b):
    return jnp.dot(a, b, preferred_element_type=F32)


def dot_t(a, b):
    return lax.dot_general(a, b, (((0,), (0,)), ((), ())), preferred_element_type=F32)


def project_kernel(own, left, right, far, sib, wk, wv, kz, vz, kzt, vzt, kf, vf):
    span = IMAGES * ROWS
    parts = [own, left, right, far] + [sib.at[j] for j in range(4)]
    for p, part in enumerate(parts):
        rows = part[...]
        kf[p * span : (p + 1) * span, :] = dot(rows, wk[...])
        vf[p * span : (p + 1) * span, :] = dot(rows, wv[...])
    zero = jnp.zeros((LAT, HD), F32)
    for i in range(IMAGES):
        for src, plain, turned in ((kf, kz, kzt), (vf, vz, vzt)):
            x = jnp.concatenate(
                [src[p * span + i * ROWS : p * span + (i + 1) * ROWS, :] for p in range(PIECES)], axis=0
            )
            top = jnp.concatenate([x[:, :HD], zero], axis=1)
            low = jnp.concatenate([zero, x[:, HD:]], axis=1)
            both = jnp.concatenate([top, low], axis=0)
            plain[i] = both.astype(BF16)
            turned[i] = both.T.astype(BF16)


def attend_kernel(blk, gain, q, c, kz, vz, kzt, vzt, att, qg, ki, acck, accv):
    scale = 1.0 / math.sqrt(HD)
    c2 = scale * math.log2(math.e)
    acck[...] = jnp.zeros_like(acck)
    accv[...] = jnp.zeros_like(accv)
    g = gain[...]

    def body(step, carry):
        base = step * UNROLL
        first = lax.broadcasted_iota(jnp.int32, (TB * UNROLL, 2 * LAT), 1) < LAT

        def halves(x, op, fill):
            a = op(jnp.where(first, x, fill), axis=1, keepdims=True)
            b = op(jnp.where(first, fill, x), axis=1, keepdims=True)
            return jnp.where(first, a, b)

        at = [pl.ds(pl.multiple_of((base + u) * TB, TB), TB) for u in range(UNROLL)]
        img = [blk[base + u] for u in range(UNROLL)]
        qs = [q[a, :] for a in at]
        gs = [(c[a, :].astype(F32) * g).astype(BF16) for a in at]
        s = jnp.concatenate([dot(qs[u], kzt[img[u]]) for u in range(UNROLL)], axis=0)
        pg = jnp.concatenate([dot(gs[u], vzt[img[u]]) for u in range(UNROLL)], axis=0)
        peak = halves(s, jnp.max, -jnp.inf)
        e = jnp.exp2((s - peak) * c2)
        prob = e / halves(e, jnp.sum, 0.0)
        low = prob.astype(BF16)
        delta = halves(prob * pg, jnp.sum, 0.0)
        sg = (prob * (pg - delta) * scale).astype(BF16)
        for u in range(UNROLL):
            lu, su = low[u * TB : (u + 1) * TB, :], sg[u * TB : (u + 1) * TB, :]
            att[at[u], :] = (dot(lu, vz[img[u]]) * g).astype(BF16)
            qg[at[u], :] = dot(su, kz[img[u]]).astype(BF16)
            kt = dot_t(su, qs[u])
            vt = dot_t(lu, gs[u])
            rows = pl.ds(pl.multiple_of(img[u] * LAT, LAT), LAT)
            acck[rows, :HD] += kt[:LAT, :HD]
            acck[rows, HD:] += kt[LAT:, HD:]
            accv[rows, :HD] += vt[:LAT, :HD]
            accv[rows, HD:] += vt[LAT:, HD:]
        return carry

    lax.fori_loop(0, blk.shape[0] // UNROLL, body, 0)
    span = IMAGES * ROWS
    for p in range(PIECES):
        for acc, lo in ((acck, 0), (accv, 2 * HD)):
            x = jnp.concatenate(
                [acc[i * LAT + p * ROWS : i * LAT + (p + 1) * ROWS, :] for i in range(IMAGES)], axis=0
            )
            ki[p * span : (p + 1) * span, lo : lo + 2 * HD] = x.astype(BF16)


def swap(x, axes, pairs):
    return lax.ppermute(x, axes, pairs)


def exchange(x, axes, **kw):
    return lax.all_to_all(x, axes, split_axis=0, concat_axis=0, tiled=True, **kw)


def body(query, latents, image_slot, block_image, key_weight, value_weight, gate, cotangent):
    seq_i, mp_i, dp_i = lax.axis_index("seq"), lax.axis_index("mp"), lax.axis_index("dp")
    tokens, width = query.shape[1], query.shape[2]
    kv = latents.shape[3]
    n_seq = 8
    cols = width // n_seq
    slots = latents.shape[1]
    half = kv // 2
    cut = latents[0].reshape(slots, PIECES, ROWS, 2, half).transpose(1, 3, 0, 2, 4)
    got = exchange(cut.reshape(16, slots * ROWS, half), ("seq", "mp"))
    mine = jnp.take(got.reshape(16 * slots, ROWS, half), image_slot[0], axis=0)
    mine = mine.reshape(IMAGES * ROWS, half)
    other = swap(mine, "mp", [(0, 1), (1, 0)])
    own = jnp.where(
        mp_i == 0, jnp.concatenate([mine, other], axis=1), jnp.concatenate([other, mine], axis=1)
    )

    def along_x(d):
        return [(x * 2 + k, ((x + d) % 4) * 2 + k) for x in range(4) for k in range(2)]

    left = swap(own, "seq", along_x(1))
    right = swap(own, "seq", along_x(-1))
    far = swap(own, "seq", along_x(2))
    here = jnp.stack([own, left, right, far])
    sib = swap(here, "seq", [(j, j ^ 1) for j in range(8)])
    wk, wv = key_weight[:, 0, :], value_weight[:, 0, :]
    shape = jax.ShapeDtypeStruct
    zs, zt = shape((IMAGES, 2 * LAT, 2 * HD), BF16), shape((IMAGES, 2 * HD, 2 * LAT), BF16)
    n_rows = IMAGES * LAT
    kz, vz, kzt, vzt = pl.pallas_call(
        project_kernel,
        out_shape=(zs, zs, zt, zt),
        in_specs=[VMEM] * 7,
        out_specs=(VMEM,) * 4,
        scratch_shapes=[pltpu.VMEM((n_rows, 2 * HD), F32)] * 2,
        compiler_params=pltpu.CompilerParams(vmem_limit_bytes=24 * 2**20),
        cost_estimate=pl.CostEstimate(
            flops=2 * n_rows * kv * 512, bytes_accessed=8 * 2**20, transcendentals=0
        ),
        name="project",
    )(own, left, right, far, sib, wk, wv)

    def to_heads(x):
        y = exchange(x[0].reshape(tokens, n_seq, cols).transpose(1, 0, 2), "seq")
        return y.reshape(n_seq * tokens, cols)

    q_all, c_all = to_heads(query), to_heads(cotangent)
    gain = jnp.repeat(jnp.tanh(lax.dynamic_slice_in_dim(gate, seq_i * 2, 2)), HD)[None, :]
    full = shape((n_seq * tokens, cols), BF16)
    att, qg, ki = pl.pallas_call(
        attend_kernel,
        out_shape=(full, full, shape((n_rows, 4 * HD), BF16)),
        in_specs=[SMEM] + [VMEM] * 7,
        out_specs=(VMEM,) * 3,
        scratch_shapes=[pltpu.VMEM((n_rows, 2 * HD), F32)] * 2,
        compiler_params=pltpu.CompilerParams(vmem_limit_bytes=24 * 2**20),
        cost_estimate=pl.CostEstimate(
            flops=2**32, bytes_accessed=11 * 2**20, transcendentals=2**19
        ),
        name="attend",
    )(block_image[0], gain, q_all, c_all, kz, vz, kzt, vzt)

    def to_tokens(x):
        y = exchange(x.reshape(n_seq, tokens, cols), "seq")
        return y.transpose(1, 0, 2).reshape(1, tokens, width)

    attended, query_grad = to_tokens(att), to_tokens(qg)

    flat = jnp.concatenate([here, sib], axis=0).reshape(n_rows, kv)
    part = dot_t(flat, ki).astype(BF16)
    rows = kv // 16
    part = part.reshape(4, 2, 2, rows, 4 * HD)
    z_i, h_i = dp_i // 2, dp_i % 2
    z_odd = z_i % 2
    pairs = []
    for z in range(8):
        for h in range(2):
            for s in range(8):
                if s % 2 == 0:
                    to = z ^ 1
                else:
                    to = (z + 1) % 8 if z % 2 else (z - 1) % 8
                pairs.append(((z * 2 + h) * 8 + s, (to * 2 + h) * 8 + s))

    def pick(x, i, axis):
        return lax.dynamic_index_in_dim(x, i, axis, keepdims=False)

    def join(x, y):
        return (x.astype(F32) + y.astype(F32)).astype(BF16)

    part = join(pick(part, z_odd, 1), swap(pick(part, 1 - z_odd, 1), ("dp", "seq"), pairs))
    part = join(pick(part, h_i, 1), swap(pick(part, 1 - h_i, 1), "dp", [(j, j ^ 1) for j in range(16)]))
    groups = [[(k * 2 + odd) * 2 + h for k in range(4)] for odd in range(2) for h in range(2)]
    total = exchange(part, "dp", axis_index_groups=groups).astype(F32).sum(axis=0)
    key_grad = total[:, : 2 * HD].reshape(rows, 1, 2 * HD)
    value_grad = total[:, 2 * HD :].reshape(rows, 1, 2 * HD)
    return attended, query_grad, key_grad, value_grad


def solution(mesh):
    in_specs = (
        P("dp", "seq", "mp"),
        P("dp", ("seq", "mp"), None, None),
        P("dp", None),
        P("dp", None),
        P(None, "mp", "seq"),
        P(None, "mp", "seq"),
        P("mp"),
        P("dp", "seq", "mp"),
    )
    out_specs = (
        P("dp", "seq", "mp"),
        P("dp", "seq", "mp"),
        P("dp", "mp", "seq"),
        P("dp", "mp", "seq"),
    )
    return jax.shard_map(body, mesh=mesh, in_specs=in_specs, out_specs=out_specs, check_vma=False)
```

```python
import math

import jax
import jax.numpy as jnp
from jax import lax
from jax.experimental import pallas as pl
from jax.experimental.pallas import tpu as pltpu
from jax.sharding import PartitionSpec as P

F32, BF16 = jnp.float32, jnp.bfloat16
IMAGES, LAT, HD, TB, UNROLL = 16, 64, 128, 32, 8
PIECES = 8
ROWS = LAT // PIECES
VMEM = pl.BlockSpec(memory_space=pltpu.VMEM)
ANY = pl.BlockSpec(memory_space=pl.ANY)
SMEM = pl.BlockSpec(memory_space=pltpu.SMEM)


def dot(a, b):
    return jnp.dot(a, b, preferred_element_type=F32)


def dot_t(a, b):
    return lax.dot_general(a, b, (((0,), (0,)), ((), ())), preferred_element_type=F32)


def fused_kernel(
    info, blk, gain, wk, wv, *refs
):
    far_parts, far_tok, (oc, send, keep) = refs[:4], refs[4:14], refs[14:17]
    (kz, vz, kzt, vzt, acck, accv, ki, gs), parts, toks, sems = refs[17:25], refs[25:29], refs[29:31], refs[31]
    a0, b0, a1, b1 = parts
    moves = list(zip(far_parts, parts))
    for r in range(8):
        for j in range(2):
            src = far_tok[5 * j + r].at[0] if r < 4 else far_tok[5 * j + 4].at[r - 4]
            moves.append((src, toks[j].at[r]))
    loads = [pltpu.make_async_copy(x, y, sems.at[n]) for n, (x, y) in enumerate(moves)]
    for x in loads:
        x.start()
    scale = 1.0 / math.sqrt(HD)
    c2 = scale * math.log2(math.e)
    me, m, odd = info[0], info[1], info[2]
    span = IMAGES * ROWS
    half = a0.shape[2]
    w_own = pl.ds(pl.multiple_of(m * half, half), half)
    w_other = pl.ds(pl.multiple_of((1 - m) * half, half), half)
    for p in range(PIECES):
        a, b = ((a0, b0), (a1, b1))[p // 4]
        if p % 4 == 0:
            loads[p // 2].wait()
            loads[p // 2 + 1].wait()
        x, y = a[p % 4], b[p % 4]
        rows = slice(p * span, (p + 1) * span)
        acck[rows, :] = dot(x, wk[w_own, :]) + dot(y, wk[w_other, :])
        accv[rows, :] = dot(x, wv[w_own, :]) + dot(y, wv[w_other, :])
    zero = jnp.zeros((LAT, HD), F32)
    for i in range(IMAGES):
        for src, plain, turned in ((acck, kz, kzt), (accv, vz, vzt)):
            x = jnp.concatenate(
                [src[p * span + i * ROWS : p * span + (i + 1) * ROWS, :] for p in range(PIECES)], axis=0
            )
            top = jnp.concatenate([x[:, :HD], zero], axis=1)
            low = jnp.concatenate([zero, x[:, HD:]], axis=1)
            both = jnp.concatenate([top, low], axis=0)
            plain[i] = both.astype(BF16)
            turned[i] = both.T.astype(BF16)
    acck[...] = jnp.zeros_like(acck)
    accv[...] = jnp.zeros_like(accv)
    g = gain[...]
    first = lax.broadcasted_iota(jnp.int32, (TB * UNROLL, 2 * LAT), 1) < LAT
    tokens = TB * UNROLL

    def halves(x, op, fill):
        a = op(jnp.where(first, x, fill), axis=1, keepdims=True)
        b = op(jnp.where(first, fill, x), axis=1, keepdims=True)
        return jnp.where(first, a, b)

    for r in range(8):
        loads[4 + 2 * r].wait()
        loads[5 + 2 * r].wait()
        own = lax.rem(me // 2 + 4 - r % 4, 4) * 2 + lax.rem(me + r // 4, 2)
        img = [blk[own * UNROLL + u] for u in range(UNROLL)]
        at = [slice(u * TB, (u + 1) * TB) for u in range(UNROLL)]
        qs = [toks[0][r, a, :] for a in at]
        gs_ = [(toks[1][r, a, :].astype(F32) * g).astype(BF16) for a in at]
        s = jnp.concatenate([dot(qs[u], kzt[img[u]]) for u in range(UNROLL)], axis=0)
        pg = jnp.concatenate([dot(gs_[u], vzt[img[u]]) for u in range(UNROLL)], axis=0)
        peak = halves(s, jnp.max, -jnp.inf)
        e = jnp.exp2((s - peak) * c2)
        prob = e / halves(e, jnp.sum, 0.0)
        low = prob.astype(BF16)
        delta = halves(prob * pg, jnp.sum, 0.0)
        sg = (prob * (pg - delta) * scale).astype(BF16)
        for u in range(UNROLL):
            lu, su = low[at[u], :], sg[at[u], :]
            oc[own, at[u], :] = (dot(lu, vz[img[u]]) * g).astype(BF16)
            oc[own, tokens + u * TB : tokens + (u + 1) * TB, :] = dot(su, kz[img[u]]).astype(BF16)
            kt = dot_t(su, qs[u])
            vt = dot_t(lu, gs_[u])
            rows = pl.ds(pl.multiple_of(img[u] * LAT, LAT), LAT)
            acck[rows, :HD] += kt[:LAT, :HD]
            acck[rows, HD:] += kt[LAT:, HD:]
            accv[rows, :HD] += vt[:LAT, :HD]
            accv[rows, HD:] += vt[LAT:, HD:]
    for p in range(PIECES):
        for acc, lo in ((acck, 0), (accv, 2 * HD)):
            x = jnp.concatenate(
                [acc[i * LAT + p * ROWS : i * LAT + (p + 1) * ROWS, :] for i in range(IMAGES)], axis=0
            )
            ki[p * span : (p + 1) * span, lo : lo + 2 * HD] = x.astype(BF16)
    for near, away, rows in ((a0, a1, w_own), (b0, b1, w_other)):
        n = 4 * span
        total = dot_t(near[...].reshape(n, half), ki[:n, :]) + dot_t(away[...].reshape(n, half), ki[n:, :])
        gs[rows, :] = total.astype(BF16)
    n = send.shape[1]
    for k in range(4):
        send[k] = gs[pl.ds(pl.multiple_of((2 * k + 1 - odd) * n, n), n), :]
        keep[k] = gs[pl.ds(pl.multiple_of((2 * k + odd) * n, n), n), :]


def rotate_kernel(info, q, c, *outs):
    cols = outs[0].shape[2]
    me = info[0]
    for d in range(4):
        for j in range(2):
            to = lax.rem(me // 2 + d, 4) * 2 + lax.rem(me + j, 2)
            off = pl.multiple_of(to * cols, cols)
            outs[d][j] = q[:, pl.ds(off, cols)]
            outs[4 + d][j] = c[:, pl.ds(off, cols)]


def spread_kernel(y, a, b):
    cols = y.shape[3]
    for r in range(8):
        a[:, r * cols : (r + 1) * cols] = y[r, 0]
        b[:, r * cols : (r + 1) * cols] = y[r, 1]


def swap(x, axes, pairs):
    return lax.ppermute(x, axes, pairs)


def exchange(x, axes, **kw):
    return lax.all_to_all(x, axes, split_axis=0, concat_axis=0, tiled=True, **kw)


def body(query, latents, image_slot, block_image, key_weight, value_weight, gate, cotangent):
    seq_i, mp_i, dp_i = lax.axis_index("seq"), lax.axis_index("mp"), lax.axis_index("dp")
    tokens, width = query.shape[1], query.shape[2]
    kv = latents.shape[3]
    n_seq = 8
    cols = width // n_seq
    slots = latents.shape[1]
    half = kv // 2
    shape = jax.ShapeDtypeStruct
    info = jnp.stack([seq_i, mp_i, dp_i // 2 % 2]).astype(jnp.int32)
    cut = latents[0].reshape(slots, PIECES, ROWS, 2, half).transpose(1, 3, 0, 2, 4)
    got = exchange(cut.reshape(16, slots * ROWS, half), ("seq", "mp"))

    def along_x(x, d):
        return swap(x, "seq", [(i * 2 + k, (i + d) % 4 * 2 + k) for i in range(4) for k in range(2)])

    def across_y(x):
        return swap(x, "mp", [(0, 1), (1, 0)])

    def sibling(x):
        return swap(x, "seq", [(j, j ^ 1) for j in range(8)])

    turned = pl.pallas_call(
        rotate_kernel,
        out_shape=[shape((2, tokens, cols), BF16)] * 8,
        in_specs=[SMEM, VMEM, VMEM],
        out_specs=[VMEM] * 8,
        name="rotate",
    )(info, query[0], cotangent[0])
    q_in = [turned[0]] + [along_x(turned[d], d) for d in range(1, 4)]
    c_in = [turned[4]] + [along_x(turned[4 + d], d) for d in range(1, 4)]
    got, q_in = lax.optimization_barrier((got, q_in))
    q_sib = sibling(jnp.stack([x[1] for x in q_in]))
    mine = jnp.take(got.reshape(16 * slots, ROWS, half), image_slot[0], axis=0)
    mine = mine.reshape(IMAGES * ROWS, half)
    own = [mine] + [along_x(mine, d) for d in (1, -1, 2)]
    other = [across_y(x) for x in own]
    other, c_in, q_sib = lax.optimization_barrier((other, c_in, q_sib))
    c_sib = sibling(jnp.stack([x[1] for x in c_in]))
    a0, b0 = jnp.stack(own), jnp.stack(other)
    a1, b1 = sibling(a0), sibling(b0)
    wk, wv = key_weight[:, 0, :], value_weight[:, 0, :]
    n_rows = IMAGES * LAT
    gain = jnp.repeat(jnp.tanh(lax.dynamic_slice_in_dim(gate, seq_i * 2, 2)), HD)[None, :]
    rows = kv // 16
    halves = shape((4, 2 * rows, 4 * HD), BF16)
    zs, zt = (IMAGES, 2 * LAT, 2 * HD), (IMAGES, 2 * HD, 2 * LAT)
    oc, send, keep = pl.pallas_call(
        fused_kernel,
        out_shape=(shape((n_seq, 2 * tokens, cols), BF16), halves, halves),
        in_specs=[SMEM, SMEM] + [VMEM] * 3 + [ANY] * 14,
        out_specs=(VMEM,) * 3,
        scratch_shapes=[pltpu.VMEM(x, BF16) for x in (zs, zs, zt, zt)]
        + [pltpu.VMEM((n_rows, 2 * HD), F32)] * 2
        + [pltpu.VMEM((n_rows, 4 * HD), BF16), pltpu.VMEM((kv, 4 * HD), BF16)]
        + [pltpu.VMEM(a0.shape, BF16)] * 4
        + [pltpu.VMEM((n_seq, tokens, cols), BF16)] * 2
        + [pltpu.SemaphoreType.DMA((20,))],
        compiler_params=pltpu.CompilerParams(vmem_limit_bytes=60 * 2**20),
        cost_estimate=pl.CostEstimate(
            flops=2**33, bytes_accessed=16 * 2**20, transcendentals=2**19
        ),
        name="fused",
    )(info, block_image[0], gain, wk, wv, a0, b0, a1, b1, *q_in, q_sib, *c_in, c_sib)

    flat_out = shape((tokens, width), BF16)
    attended, query_grad = pl.pallas_call(
        spread_kernel,
        grid=(tokens // 64,),
        out_shape=(flat_out, flat_out),
        in_specs=[pl.BlockSpec((n_seq, 2, 64, cols), lambda t: (0, 0, t, 0))],
        out_specs=[pl.BlockSpec((64, width), lambda t: (t, 0))] * 2,
        name="spread",
    )(exchange(oc, "seq").reshape(n_seq, 2, tokens, cols))

    z_i, h_i = dp_i // 2, dp_i % 2
    pairs = []
    for z in range(8):
        for h in range(2):
            for s in range(8):
                if s % 2 == 0:
                    to = z ^ 1
                else:
                    to = (z + 1) % 8 if z % 2 else (z - 1) % 8
                pairs.append(((z * 2 + h) * 8 + s, (to * 2 + h) * 8 + s))

    def pick(x, i, axis):
        return lax.dynamic_index_in_dim(x, i, axis, keepdims=False)

    def join(x, y):
        return (x.astype(F32) + y.astype(F32)).astype(BF16)

    part = join(keep, swap(send, ("dp", "seq"), pairs)).reshape(4, 2, rows, 4 * HD)
    part = join(pick(part, h_i, 1), swap(pick(part, 1 - h_i, 1), "dp", [(j, j ^ 1) for j in range(16)]))
    k_i = z_i // 2
    more = []
    for r in range(1, 4):
        perm = [(z * 2 + h, (z + 2 * r) % 8 * 2 + h) for z in range(8) for h in range(2)]
        more.append(swap(pick(part, (k_i + r) % 4, 0), "dp", perm))
    (attended, query_grad), more = lax.optimization_barrier(((attended, query_grad), more))
    total = pick(part, k_i, 0).astype(F32)
    for x in more:
        total = total + x.astype(F32)
    key_grad = total[:, : 2 * HD].reshape(rows, 1, 2 * HD)
    value_grad = total[:, 2 * HD :].reshape(rows, 1, 2 * HD)
    return attended[None], query_grad[None], key_grad, value_grad


def solution(mesh):
    in_specs = (
        P("dp", "seq", "mp"),
        P("dp", ("seq", "mp"), None, None),
        P("dp", None),
        P("dp", None),
        P(None, "mp", "seq"),
        P(None, "mp", "seq"),
        P("mp"),
        P("dp", "seq", "mp"),
    )
    out_specs = (
        P("dp", "seq", "mp"),
        P("dp", "seq", "mp"),
        P("dp", "mp", "seq"),
        P("dp", "mp", "seq"),
    )
    return jax.shard_map(body, mesh=mesh, in_specs=in_specs, out_specs=out_specs, check_vma=False)
```

```python
import math

import jax
import jax.numpy as jnp
from jax import lax
from jax.experimental import pallas as pl
from jax.experimental.pallas import tpu as pltpu
from jax.sharding import PartitionSpec as P

F32, BF16 = jnp.float32, jnp.bfloat16
IMAGES, LAT, HD, TB, UNROLL = 16, 64, 128, 32, 8
PIECES = 8
ROWS = LAT // PIECES
VMEM = pl.BlockSpec(memory_space=pltpu.VMEM)
ANY = pl.BlockSpec(memory_space=pl.ANY)
SMEM = pl.BlockSpec(memory_space=pltpu.SMEM)


def dot(a, b):
    return jnp.dot(a, b, preferred_element_type=F32)


def dot_t(a, b):
    return lax.dot_general(a, b, (((0,), (0,)), ((), ())), preferred_element_type=F32)


def fused_kernel(
    info, blk, gain, wk, wv, *refs
):
    far_parts, far_tok, (oc, send, keep) = refs[:4], refs[4:14], refs[14:17]
    (kz, vz, kzt, vzt, acck, accv, ki, gs), parts, toks, made, sems = refs[17:25], refs[25:29], refs[29:31], *refs[31:33]
    ss, pgs, lows, sgs = refs[33:]
    a0, b0, a1, b1 = parts
    moves = list(zip(far_parts, parts))
    for r in range(8):
        for j in range(2):
            src = far_tok[5 * j + r].at[0] if r < 4 else far_tok[5 * j + 4].at[r - 4]
            moves.append((src, toks[j].at[r]))
    loads = [pltpu.make_async_copy(x, y, sems.at[n]) for n, (x, y) in enumerate(moves)]
    for x in loads:
        x.start()
    scale = 1.0 / math.sqrt(HD)
    c2 = scale * math.log2(math.e)
    me, m, odd = info[0], info[1], info[2]
    span = IMAGES * ROWS
    half = a0.shape[2]
    w_own = pl.ds(pl.multiple_of(m * half, half), half)
    w_other = pl.ds(pl.multiple_of((1 - m) * half, half), half)
    for n, (a, b) in enumerate(((a0, b0), (a1, b1))):
        loads[2 * n].wait()
        loads[2 * n + 1].wait()
        x, y = a[...].reshape(4 * span, half), b[...].reshape(4 * span, half)
        rows = slice(n * 4 * span, (n + 1) * 4 * span)
        acck[rows, :] = dot(x, wk[w_own, :]) + dot(y, wk[w_other, :])
        accv[rows, :] = dot(x, wv[w_own, :]) + dot(y, wv[w_other, :])
    zero = jnp.zeros((LAT, HD), F32)
    for i in range(IMAGES):
        for src, plain, turned in ((acck, kz, kzt), (accv, vz, vzt)):
            x = jnp.concatenate(
                [src[p * span + i * ROWS : p * span + (i + 1) * ROWS, :] for p in range(PIECES)], axis=0
            )
            top = jnp.concatenate([x[:, :HD], zero], axis=1)
            low = jnp.concatenate([zero, x[:, HD:]], axis=1)
            both = jnp.concatenate([top, low], axis=0)
            plain[i] = both.astype(BF16)
            turned[i] = both.T.astype(BF16)
    acck[...] = jnp.zeros_like(acck)
    accv[...] = jnp.zeros_like(accv)
    g = gain[...]
    first = lax.broadcasted_iota(jnp.int32, (TB * UNROLL, 2 * LAT), 1) < LAT
    tokens = TB * UNROLL

    ones = lax.broadcasted_iota(jnp.int32, (2 * LAT, 2 * LAT), 0) // LAT
    ones = (ones == lax.broadcasted_iota(jnp.int32, (2 * LAT, 2 * LAT), 1) // LAT).astype(BF16)

    def half_max(x):
        a = jnp.max(jnp.where(first, x, -jnp.inf), axis=1, keepdims=True)
        b = jnp.max(jnp.where(first, -jnp.inf, x), axis=1, keepdims=True)
        return jnp.where(first, a, b)

    def half_sum(x):
        high = x.astype(BF16)
        low = (x - high.astype(F32)).astype(BF16)
        return dot(high, ones) + dot(low, ones)

    for x in loads[4:]:
        x.wait()

    at = [slice(u * TB, (u + 1) * TB) for u in range(UNROLL)]

    def owner(r):
        return lax.rem(me // 2 + 4 - r % 4, 4) * 2 + lax.rem(me + r // 4, 2)

    def images(r):
        return [blk[owner(r) * UNROLL + u] for u in range(UNROLL)]

    def scores(r):
        img = images(r)
        toks[1][r] = (toks[1][r].astype(F32) * g).astype(BF16)
        for rows, mats, out in ((toks[0], kzt, ss), (toks[1], vzt, pgs)):
            for u in range(0, UNROLL, 2):
                pair = jnp.concatenate([mats[img[u]], mats[img[u + 1]]], axis=1)
                both = dot(rows[r, u * TB : (u + 2) * TB, :], pair)
                out[r, at[u], :] = both[:TB, : 2 * LAT]
                out[r, at[u + 1], :] = both[TB:, 2 * LAT :]

    def weigh(r):
        s, pg = ss[r], pgs[r]
        e = jnp.exp2((s - half_max(s)) * c2)
        prob = e / half_sum(e)
        lows[r] = prob.astype(BF16)
        delta = half_sum(prob * pg)
        sgs[r] = (prob * (pg - delta) * scale).astype(BF16)

    def collect(r):
        img = images(r)
        for u in range(UNROLL):
            lu, su = lows[r, at[u], :], sgs[r, at[u], :]
            made[r, at[u], :] = (dot(lu, vz[img[u]]) * g).astype(BF16)
            made[r, tokens + u * TB : tokens + (u + 1) * TB, :] = dot(su, kz[img[u]]).astype(BF16)
            kt = dot_t(su, toks[0][r, at[u], :])
            vt = dot_t(lu, toks[1][r, at[u], :])
            rows = pl.ds(pl.multiple_of(img[u] * LAT, LAT), LAT)
            acck[rows, :HD] += kt[:LAT, :HD]
            acck[rows, HD:] += kt[LAT:, HD:]
            accv[rows, :HD] += vt[:LAT, :HD]
            accv[rows, HD:] += vt[LAT:, HD:]

    for step in range(10):
        if step < 8:
            scores(step)
        if 1 <= step < 9:
            weigh(step - 1)
        if step >= 2:
            collect(step - 2)
    stores = [pltpu.make_async_copy(made.at[r], oc.at[owner(r)], sems.at[20 + r]) for r in range(8)]
    for x in stores:
        x.start()
    for p in range(PIECES):
        for acc, lo in ((acck, 0), (accv, 2 * HD)):
            x = jnp.concatenate(
                [acc[i * LAT + p * ROWS : i * LAT + (p + 1) * ROWS, :] for i in range(IMAGES)], axis=0
            )
            ki[p * span : (p + 1) * span, lo : lo + 2 * HD] = x.astype(BF16)
    for near, away, rows in ((a0, a1, w_own), (b0, b1, w_other)):
        n = 4 * span
        total = dot_t(near[...].reshape(n, half), ki[:n, :]) + dot_t(away[...].reshape(n, half), ki[n:, :])
        gs[rows, :] = total.astype(BF16)
    n = send.shape[1]
    for k in range(4):
        send[k] = gs[pl.ds(pl.multiple_of((2 * k + 1 - odd) * n, n), n), :]
        keep[k] = gs[pl.ds(pl.multiple_of((2 * k + odd) * n, n), n), :]
    for x in stores:
        x.wait()


def rotate_kernel(info, q, c, *outs):
    cols = outs[0].shape[2]
    me = info[0]
    for d in range(4):
        for j in range(2):
            to = lax.rem(me // 2 + d, 4) * 2 + lax.rem(me + j, 2)
            off = pl.multiple_of(to * cols, cols)
            outs[d][j] = q[:, pl.ds(off, cols)]
            outs[4 + d][j] = c[:, pl.ds(off, cols)]


def spread_kernel(y, a, b):
    cols = y.shape[3]
    for r in range(8):
        a[:, r * cols : (r + 1) * cols] = y[r, 0]
        b[:, r * cols : (r + 1) * cols] = y[r, 1]


def swap(x, axes, pairs):
    return lax.ppermute(x, axes, pairs)


def exchange(x, axes, **kw):
    return lax.all_to_all(x, axes, split_axis=0, concat_axis=0, tiled=True, **kw)


def body(query, latents, image_slot, block_image, key_weight, value_weight, gate, cotangent):
    seq_i, mp_i, dp_i = lax.axis_index("seq"), lax.axis_index("mp"), lax.axis_index("dp")
    tokens, width = query.shape[1], query.shape[2]
    kv = latents.shape[3]
    n_seq = 8
    cols = width // n_seq
    slots = latents.shape[1]
    half = kv // 2
    shape = jax.ShapeDtypeStruct
    info = jnp.stack([seq_i, mp_i, dp_i // 2 % 2]).astype(jnp.int32)
    cut = latents[0].reshape(slots, PIECES, ROWS, 2, half).transpose(1, 3, 0, 2, 4)
    got = exchange(cut.reshape(16, slots * ROWS, half), ("seq", "mp"))

    def along_x(x, d):
        return swap(x, "seq", [(i * 2 + k, (i + d) % 4 * 2 + k) for i in range(4) for k in range(2)])

    def across_y(x):
        return swap(x, "mp", [(0, 1), (1, 0)])

    def sibling(x):
        return swap(x, "seq", [(j, j ^ 1) for j in range(8)])

    turned = pl.pallas_call(
        rotate_kernel,
        out_shape=[shape((2, tokens, cols), BF16)] * 8,
        in_specs=[SMEM, VMEM, VMEM],
        out_specs=[VMEM] * 8,
        name="rotate",
    )(info, query[0], cotangent[0])
    q_in = [turned[0]] + [along_x(turned[d], d) for d in range(1, 4)]
    got, q_in[1], q_in[3] = lax.optimization_barrier((got, q_in[1], q_in[3]))
    mine = jnp.take(got.reshape(16 * slots, ROWS, half), image_slot[0], axis=0)
    mine = mine.reshape(IMAGES * ROWS, half)
    own = [mine] + [along_x(mine, d) for d in (1, -1, 2)]
    other = [across_y(x) for x in own]
    held, c_out = lax.optimization_barrier((own[1:], turned[4:]))
    c_in = [c_out[0]] + [along_x(c_out[d], d) for d in range(1, 4)]
    q_sib = sibling(jnp.stack([x[1] for x in q_in]))
    other, c_in, q_sib = lax.optimization_barrier((other, c_in, q_sib))
    c_sib = sibling(jnp.stack([x[1] for x in c_in]))
    a0, b0 = jnp.stack(own), jnp.stack(other)
    a1, b1 = sibling(a0), sibling(b0)
    wk, wv = key_weight[:, 0, :], value_weight[:, 0, :]
    n_rows = IMAGES * LAT
    gain = jnp.repeat(jnp.tanh(lax.dynamic_slice_in_dim(gate, seq_i * 2, 2)), HD)[None, :]
    rows = kv // 16
    halves = shape((4, 2 * rows, 4 * HD), BF16)
    zs, zt = (IMAGES, 2 * LAT, 2 * HD), (IMAGES, 2 * HD, 2 * LAT)
    oc, send, keep = pl.pallas_call(
        fused_kernel,
        out_shape=(shape((n_seq, 2 * tokens, cols), BF16), halves, halves),
        in_specs=[SMEM, SMEM] + [VMEM] * 3 + [ANY] * 14,
        out_specs=(ANY, VMEM, VMEM),
        scratch_shapes=[pltpu.VMEM(x, BF16) for x in (zs, zs, zt, zt)]
        + [pltpu.VMEM((n_rows, 2 * HD), F32)] * 2
        + [pltpu.VMEM((n_rows, 4 * HD), BF16), pltpu.VMEM((kv, 4 * HD), BF16)]
        + [pltpu.VMEM(a0.shape, BF16)] * 4
        + [pltpu.VMEM((n_seq, tokens, cols), BF16)] * 2
        + [pltpu.VMEM((n_seq, 2 * tokens, cols), BF16), pltpu.SemaphoreType.DMA((28,))]
        + [pltpu.VMEM((n_seq, tokens, 2 * LAT), x) for x in (F32, F32, BF16, BF16)],
        compiler_params=pltpu.CompilerParams(vmem_limit_bytes=26 * 2**20),
        cost_estimate=pl.CostEstimate(
            flops=2**33, bytes_accessed=16 * 2**20, transcendentals=2**19
        ),
        name="fused",
    )(info, block_image[0], gain, wk, wv, a0, b0, a1, b1, *q_in, q_sib, *c_in, c_sib)

    flat_out = shape((tokens, width), BF16)
    attended, query_grad = pl.pallas_call(
        spread_kernel,
        grid=(tokens // 64,),
        out_shape=(flat_out, flat_out),
        in_specs=[pl.BlockSpec((n_seq, 2, 64, cols), lambda t: (0, 0, t, 0))],
        out_specs=[pl.BlockSpec((64, width), lambda t: (t, 0))] * 2,
        name="spread",
    )(exchange(oc, "seq").reshape(n_seq, 2, tokens, cols))

    z_i, h_i = dp_i // 2, dp_i % 2
    pairs = []
    for z in range(8):
        for h in range(2):
            for s in range(8):
                if s % 2 == 0:
                    to = z ^ 1
                else:
                    to = (z + 1) % 8 if z % 2 else (z - 1) % 8
                pairs.append(((z * 2 + h) * 8 + s, (to * 2 + h) * 8 + s))

    def pick(x, i, axis):
        return lax.dynamic_index_in_dim(x, i, axis, keepdims=False)

    def join(x, y):
        return (x.astype(F32) + y.astype(F32)).astype(BF16)

    part = join(keep, swap(send, ("dp", "seq"), pairs)).reshape(4, 2, rows, 4 * HD)
    part = join(pick(part, h_i, 1), swap(pick(part, 1 - h_i, 1), "dp", [(j, j ^ 1) for j in range(16)]))
    k_i = z_i // 2
    more = []
    for r in range(1, 4):
        perm = [(z * 2 + h, (z + 2 * r) % 8 * 2 + h) for z in range(8) for h in range(2)]
        more.append(swap(pick(part, (k_i + r) % 4, 0), "dp", perm))
    (attended, query_grad), more = lax.optimization_barrier(((attended, query_grad), more))
    total = pick(part, k_i, 0).astype(F32)
    for x in more:
        total = total + x.astype(F32)
    key_grad = total[:, : 2 * HD].reshape(rows, 1, 2 * HD)
    value_grad = total[:, 2 * HD :].reshape(rows, 1, 2 * HD)
    return attended[None], query_grad[None], key_grad, value_grad


def solution(mesh):
    in_specs = (
        P("dp", "seq", "mp"),
        P("dp", ("seq", "mp"), None, None),
        P("dp", None),
        P("dp", None),
        P(None, "mp", "seq"),
        P(None, "mp", "seq"),
        P("mp"),
        P("dp", "seq", "mp"),
    )
    out_specs = (
        P("dp", "seq", "mp"),
        P("dp", "seq", "mp"),
        P("dp", "mp", "seq"),
        P("dp", "mp", "seq"),
    )
    return jax.shard_map(body, mesh=mesh, in_specs=in_specs, out_specs=out_specs, check_vma=False)
```

```python
import math

import jax
import jax.numpy as jnp
from jax import lax
from jax.experimental import pallas as pl
from jax.experimental.pallas import tpu as pltpu
from jax.sharding import PartitionSpec as P

F32, BF16 = jnp.float32, jnp.bfloat16
IMAGES, LAT, HD, TB, UNROLL = 16, 64, 128, 32, 8
PIECES = 8
ROWS = LAT // PIECES
VMEM = pl.BlockSpec(memory_space=pltpu.VMEM)
ANY = pl.BlockSpec(memory_space=pl.ANY)
SMEM = pl.BlockSpec(memory_space=pltpu.SMEM)


def dot(a, b):
    return jnp.dot(a, b, preferred_element_type=F32)


def dot_t(a, b):
    return lax.dot_general(a, b, (((0,), (0,)), ((), ())), preferred_element_type=F32)


def fused_kernel(
    info, blk, gain, wk, wv, *refs
):
    far_parts, far_tok, (oc, send, keep) = refs[:4], refs[4:14], refs[14:17]
    (kz, vz, kzt, vzt, acck, accv, ki, gs), parts, toks, made, sems = refs[17:25], refs[25:29], refs[29:31], *refs[31:33]
    ss, pgs, lows, sgs = refs[33:]
    a0, b0, a1, b1 = parts
    moves = list(zip(far_parts, parts))
    for r in range(8):
        for j in range(2):
            src = far_tok[5 * j + r].at[0] if r < 4 else far_tok[5 * j + 4].at[r - 4]
            moves.append((src, toks[j].at[r]))
    loads = [pltpu.make_async_copy(x, y, sems.at[n]) for n, (x, y) in enumerate(moves)]
    for x in loads:
        x.start()
    scale = 1.0 / math.sqrt(HD)
    c2 = scale * math.log2(math.e)
    me, m, odd = info[0], info[1], info[2]
    span = IMAGES * ROWS
    half = a0.shape[2]
    w_own = pl.ds(pl.multiple_of(m * half, half), half)
    w_other = pl.ds(pl.multiple_of((1 - m) * half, half), half)
    for n, (a, b) in enumerate(((a0, b0), (a1, b1))):
        loads[2 * n].wait()
        loads[2 * n + 1].wait()
        x, y = a[...].reshape(4 * span, half), b[...].reshape(4 * span, half)
        rows = slice(n * 4 * span, (n + 1) * 4 * span)
        acck[rows, :] = dot(x, wk[w_own, :]) + dot(y, wk[w_other, :])
        accv[rows, :] = dot(x, wv[w_own, :]) + dot(y, wv[w_other, :])
    zero = jnp.zeros((LAT, HD), F32)
    for i in range(IMAGES):
        for src, plain, turned in ((acck, kz, kzt), (accv, vz, vzt)):
            x = jnp.concatenate(
                [src[p * span + i * ROWS : p * span + (i + 1) * ROWS, :] for p in range(PIECES)], axis=0
            )
            top = jnp.concatenate([x[:, :HD], zero], axis=1)
            low = jnp.concatenate([zero, x[:, HD:]], axis=1)
            both = jnp.concatenate([top, low], axis=0)
            plain[i] = both.astype(BF16)
            turned[i] = both.T.astype(BF16)
    acck[...] = jnp.zeros_like(acck)
    accv[...] = jnp.zeros_like(accv)
    g = gain[...]
    first = lax.broadcasted_iota(jnp.int32, (TB * UNROLL, 2 * LAT), 1) < LAT
    tokens = TB * UNROLL

    ones = lax.broadcasted_iota(jnp.int32, (2 * LAT, 2 * LAT), 0) // LAT
    ones = (ones == lax.broadcasted_iota(jnp.int32, (2 * LAT, 2 * LAT), 1) // LAT).astype(BF16)

    def half_max(x):
        a = jnp.max(jnp.where(first, x, -jnp.inf), axis=1, keepdims=True)
        b = jnp.max(jnp.where(first, -jnp.inf, x), axis=1, keepdims=True)
        return jnp.where(first, a, b)

    def half_sum(x):
        high = x.astype(BF16)
        low = (x - high.astype(F32)).astype(BF16)
        return dot(high, ones) + dot(low, ones)

    for x in loads[4:]:
        x.wait()

    at = [slice(u * TB, (u + 1) * TB) for u in range(UNROLL)]

    def owner(r):
        return lax.rem(me // 2 + 4 - r % 4, 4) * 2 + lax.rem(me + r // 4, 2)

    def images(r):
        return [blk[owner(r) * UNROLL + u] for u in range(UNROLL)]

    def scores(r):
        img = images(r)
        toks[1][r] = (toks[1][r].astype(F32) * g).astype(BF16)
        for rows, mats, out in ((toks[0], kzt, ss), (toks[1], vzt, pgs)):
            for u in range(0, UNROLL, 2):
                pair = jnp.concatenate([mats[img[u]], mats[img[u + 1]]], axis=1)
                both = dot(rows[r, u * TB : (u + 2) * TB, :], pair)
                out[r, at[u], :] = both[:TB, : 2 * LAT]
                out[r, at[u + 1], :] = both[TB:, 2 * LAT :]

    def weigh(r):
        s, pg = ss[r], pgs[r]
        e = jnp.exp2((s - half_max(s)) * c2)
        prob = e / half_sum(e)
        lows[r] = prob.astype(BF16)
        delta = half_sum(prob * pg)
        sgs[r] = (prob * (pg - delta) * scale).astype(BF16)

    def collect(r):
        img = images(r)
        for u in range(UNROLL):
            lu, su = lows[r, at[u], :], sgs[r, at[u], :]
            made[r, at[u], :] = (dot(lu, vz[img[u]]) * g).astype(BF16)
            made[r, tokens + u * TB : tokens + (u + 1) * TB, :] = dot(su, kz[img[u]]).astype(BF16)
            kt = dot_t(su, toks[0][r, at[u], :])
            vt = dot_t(lu, toks[1][r, at[u], :])
            rows = pl.ds(pl.multiple_of(img[u] * LAT, LAT), LAT)
            acck[rows, :HD] += kt[:LAT, :HD]
            acck[rows, HD:] += kt[LAT:, HD:]
            accv[rows, :HD] += vt[:LAT, :HD]
            accv[rows, HD:] += vt[LAT:, HD:]

    for step in range(10):
        if step < 8:
            scores(step)
        if 1 <= step < 9:
            weigh(step - 1)
        if step >= 2:
            collect(step - 2)
    stores = [pltpu.make_async_copy(made.at[r], oc.at[owner(r)], sems.at[20 + r]) for r in range(8)]
    for x in stores:
        x.start()
    for p in range(PIECES):
        for acc, lo in ((acck, 0), (accv, 2 * HD)):
            x = jnp.concatenate(
                [acc[i * LAT + p * ROWS : i * LAT + (p + 1) * ROWS, :] for i in range(IMAGES)], axis=0
            )
            ki[p * span : (p + 1) * span, lo : lo + 2 * HD] = x.astype(BF16)
    for near, away, rows in ((a0, a1, w_own), (b0, b1, w_other)):
        n = 4 * span
        total = dot_t(near[...].reshape(n, half), ki[:n, :]) + dot_t(away[...].reshape(n, half), ki[n:, :])
        gs[rows, :] = total.astype(BF16)
    n = send.shape[1]
    for k in range(4):
        send[k] = gs[pl.ds(pl.multiple_of((2 * k + 1 - odd) * n, n), n), :]
        keep[k] = gs[pl.ds(pl.multiple_of((2 * k + odd) * n, n), n), :]
    for x in stores:
        x.wait()


def rotate_kernel(info, q, c, *outs):
    cols = outs[0].shape[2]
    me = info[0]
    for d in range(4):
        for j in range(2):
            to = lax.rem(me // 2 + d, 4) * 2 + lax.rem(me + j, 2)
            off = pl.multiple_of(to * cols, cols)
            outs[d][j] = q[:, pl.ds(off, cols)]
            outs[4 + d][j] = c[:, pl.ds(off, cols)]


def spread_kernel(y, a, b):
    cols = y.shape[3]
    for r in range(8):
        a[:, r * cols : (r + 1) * cols] = y[r, 0]
        b[:, r * cols : (r + 1) * cols] = y[r, 1]


def swap(x, axes, pairs):
    return lax.ppermute(x, axes, pairs)


def exchange(x, axes, **kw):
    return lax.all_to_all(x, axes, split_axis=0, concat_axis=0, tiled=True, **kw)


def body(query, latents, image_slot, block_image, key_weight, value_weight, gate, cotangent):
    seq_i, mp_i, dp_i = lax.axis_index("seq"), lax.axis_index("mp"), lax.axis_index("dp")
    tokens, width = query.shape[1], query.shape[2]
    kv = latents.shape[3]
    n_seq = 8
    cols = width // n_seq
    slots = latents.shape[1]
    half = kv // 2
    shape = jax.ShapeDtypeStruct
    info = jnp.stack([seq_i, mp_i, dp_i // 2 % 2]).astype(jnp.int32)
    cut = latents[0].reshape(slots, PIECES, ROWS, 2, half).transpose(1, 3, 0, 2, 4)
    got = exchange(cut.reshape(16, slots * ROWS, half), ("seq", "mp"))

    def along_x(x, d):
        return swap(x, "seq", [(i * 2 + k, (i + d) % 4 * 2 + k) for i in range(4) for k in range(2)])

    def across_y(x):
        return swap(x, "mp", [(0, 1), (1, 0)])

    def sibling(x):
        return swap(x, "seq", [(j, j ^ 1) for j in range(8)])

    turned = pl.pallas_call(
        rotate_kernel,
        out_shape=[shape((2, tokens, cols), BF16)] * 8,
        in_specs=[SMEM, VMEM, VMEM],
        out_specs=[VMEM] * 8,
        name="rotate",
    )(info, query[0], cotangent[0])
    q_in = [turned[0], along_x(turned[1], 1), None, along_x(turned[3], 3)]
    got, q_in[1], q_in[3] = lax.optimization_barrier((got, q_in[1], q_in[3]))
    mine = jnp.take(got.reshape(16 * slots, ROWS, half), image_slot[0], axis=0)
    mine, q_far = lax.optimization_barrier((mine.reshape(IMAGES * ROWS, half), turned[2]))
    moved = [along_x(mine, d) for d in (1, -1, 2)]
    q_in[2] = along_x(q_far, 2)
    first = across_y(mine)
    moved, first, c_out = lax.optimization_barrier((moved, first, turned[4:]))
    c_in = [c_out[0]] + [along_x(c_out[d], d) for d in range(1, 4)]
    own, other = [mine] + moved, [first] + [across_y(x) for x in moved]
    q_in, c_in[1:], other[1:] = lax.optimization_barrier((q_in, c_in[1:], other[1:]))
    q_sib = sibling(jnp.stack([x[1] for x in q_in]))
    other, c_in, q_sib = lax.optimization_barrier((other, c_in, q_sib))
    c_sib = sibling(jnp.stack([x[1] for x in c_in]))
    a0, b0 = jnp.stack(own), jnp.stack(other)
    a1, b1 = sibling(a0), sibling(b0)
    wk, wv = key_weight[:, 0, :], value_weight[:, 0, :]
    n_rows = IMAGES * LAT
    gain = jnp.repeat(jnp.tanh(lax.dynamic_slice_in_dim(gate, seq_i * 2, 2)), HD)[None, :]
    rows = kv // 16
    halves = shape((4, 2 * rows, 4 * HD), BF16)
    zs, zt = (IMAGES, 2 * LAT, 2 * HD), (IMAGES, 2 * HD, 2 * LAT)
    oc, send, keep = pl.pallas_call(
        fused_kernel,
        out_shape=(shape((n_seq, 2 * tokens, cols), BF16), halves, halves),
        in_specs=[SMEM, SMEM] + [VMEM] * 3 + [ANY] * 14,
        out_specs=(ANY, VMEM, VMEM),
        scratch_shapes=[pltpu.VMEM(x, BF16) for x in (zs, zs, zt, zt)]
        + [pltpu.VMEM((n_rows, 2 * HD), F32)] * 2
        + [pltpu.VMEM((n_rows, 4 * HD), BF16), pltpu.VMEM((kv, 4 * HD), BF16)]
        + [pltpu.VMEM(a0.shape, BF16)] * 4
        + [pltpu.VMEM((n_seq, tokens, cols), BF16)] * 2
        + [pltpu.VMEM((n_seq, 2 * tokens, cols), BF16), pltpu.SemaphoreType.DMA((28,))]
        + [pltpu.VMEM((n_seq, tokens, 2 * LAT), x) for x in (F32, F32, BF16, BF16)],
        compiler_params=pltpu.CompilerParams(vmem_limit_bytes=60 * 2**20),
        cost_estimate=pl.CostEstimate(
            flops=2**33, bytes_accessed=16 * 2**20, transcendentals=2**19
        ),
        name="fused",
    )(info, block_image[0], gain, wk, wv, a0, b0, a1, b1, *q_in, q_sib, *c_in, c_sib)

    flat_out = shape((tokens, width), BF16)
    attended, query_grad = pl.pallas_call(
        spread_kernel,
        grid=(tokens // 64,),
        out_shape=(flat_out, flat_out),
        in_specs=[pl.BlockSpec((n_seq, 2, 64, cols), lambda t: (0, 0, t, 0))],
        out_specs=[pl.BlockSpec((64, width), lambda t: (t, 0))] * 2,
        name="spread",
    )(exchange(oc, "seq").reshape(n_seq, 2, tokens, cols))

    z_i, h_i = dp_i // 2, dp_i % 2
    pairs = []
    for z in range(8):
        for h in range(2):
            for s in range(8):
                if s % 2 == 0:
                    to = z ^ 1
                else:
                    to = (z + 1) % 8 if z % 2 else (z - 1) % 8
                pairs.append(((z * 2 + h) * 8 + s, (to * 2 + h) * 8 + s))

    def pick(x, i, axis):
        return lax.dynamic_index_in_dim(x, i, axis, keepdims=False)

    def join(x, y):
        return (x.astype(F32) + y.astype(F32)).astype(BF16)

    part = join(keep, swap(send, ("dp", "seq"), pairs)).reshape(4, 2, rows, 4 * HD)
    part = join(pick(part, h_i, 1), swap(pick(part, 1 - h_i, 1), "dp", [(j, j ^ 1) for j in range(16)]))
    k_i = z_i // 2
    more = []
    for r in range(1, 4):
        perm = [(z * 2 + h, (z + 2 * r) % 8 * 2 + h) for z in range(8) for h in range(2)]
        more.append(swap(pick(part, (k_i + r) % 4, 0), "dp", perm))
    (attended, query_grad), more = lax.optimization_barrier(((attended, query_grad), more))
    total = pick(part, k_i, 0).astype(F32)
    for x in more:
        total = total + x.astype(F32)
    key_grad = total[:, : 2 * HD].reshape(rows, 1, 2 * HD)
    value_grad = total[:, 2 * HD :].reshape(rows, 1, 2 * HD)
    return attended[None], query_grad[None], key_grad, value_grad


def solution(mesh):
    in_specs = (
        P("dp", "seq", "mp"),
        P("dp", ("seq", "mp"), None, None),
        P("dp", None),
        P("dp", None),
        P(None, "mp", "seq"),
        P(None, "mp", "seq"),
        P("mp"),
        P("dp", "seq", "mp"),
    )
    out_specs = (
        P("dp", "seq", "mp"),
        P("dp", "seq", "mp"),
        P("dp", "mp", "seq"),
        P("dp", "mp", "seq"),
    )
    return jax.shard_map(body, mesh=mesh, in_specs=in_specs, out_specs=out_specs, check_vma=False)
```

```python
import math

import jax
import jax.numpy as jnp
from jax import lax
from jax.experimental import pallas as pl
from jax.experimental.pallas import tpu as pltpu
from jax.sharding import PartitionSpec as P

F32, BF16 = jnp.float32, jnp.bfloat16
IMAGES, LAT, HD, TB, UNROLL = 16, 64, 128, 32, 8
PIECES = 8
ROWS = LAT // PIECES
VMEM = pl.BlockSpec(memory_space=pltpu.VMEM)
ANY = pl.BlockSpec(memory_space=pl.ANY)
SMEM = pl.BlockSpec(memory_space=pltpu.SMEM)


def dot(a, b):
    return jnp.dot(a, b, preferred_element_type=F32)


def dot_t(a, b):
    return lax.dot_general(a, b, (((0,), (0,)), ((), ())), preferred_element_type=F32)


def fused_kernel(
    info, blk, gain, wk, wv, *refs
):
    far_parts, far_tok, (oc, lead, rest, keep) = refs[:4], refs[4:13], refs[13:17]
    (kz, vz, kzt, vzt, acck, accv, ki, gs), parts, toks, made, sems = refs[17:25], refs[25:29], refs[29:31], *refs[31:33]
    ss, pgs, lows, sgs = refs[33:]
    a0, b0, a1, b1 = parts
    moves = list(zip(far_parts, parts))
    for r in range(8):
        moves.append((far_tok[r].at[0] if r < 4 else far_tok[4].at[r - 4], toks[0].at[r]))
        moves.append((far_tok[5 + r % 4].at[r // 4], toks[1].at[r]))
    loads = [pltpu.make_async_copy(x, y, sems.at[n]) for n, (x, y) in enumerate(moves)]
    for x in loads:
        x.start()
    scale = 1.0 / math.sqrt(HD)
    c2 = scale * math.log2(math.e)
    me, m, odd = info[0], info[1], info[2]
    span = IMAGES * ROWS
    half = a0.shape[2]
    w_own = pl.ds(pl.multiple_of(m * half, half), half)
    w_other = pl.ds(pl.multiple_of((1 - m) * half, half), half)
    for n, (a, b) in enumerate(((a0, b0), (a1, b1))):
        loads[2 * n].wait()
        loads[2 * n + 1].wait()
        x, y = a[...].reshape(4 * span, half), b[...].reshape(4 * span, half)
        rows = slice(n * 4 * span, (n + 1) * 4 * span)
        acck[rows, :] = dot(x, wk[w_own, :]) + dot(y, wk[w_other, :])
        accv[rows, :] = dot(x, wv[w_own, :]) + dot(y, wv[w_other, :])
    zero = jnp.zeros((LAT, HD), F32)
    for i in range(IMAGES):
        for src, plain, turned in ((acck, kz, kzt), (accv, vz, vzt)):
            x = jnp.concatenate(
                [src[p * span + i * ROWS : p * span + (i + 1) * ROWS, :] for p in range(PIECES)], axis=0
            )
            top = jnp.concatenate([x[:, :HD], zero], axis=1)
            low = jnp.concatenate([zero, x[:, HD:]], axis=1)
            both = jnp.concatenate([top, low], axis=0)
            plain[i] = both.astype(BF16)
            turned[i] = both.T.astype(BF16)
    acck[...] = jnp.zeros_like(acck)
    accv[...] = jnp.zeros_like(accv)
    g = gain[...]
    first = lax.broadcasted_iota(jnp.int32, (TB * UNROLL, 2 * LAT), 1) < LAT
    tokens = TB * UNROLL

    ones = lax.broadcasted_iota(jnp.int32, (2 * LAT, 2 * LAT), 0) // LAT
    ones = (ones == lax.broadcasted_iota(jnp.int32, (2 * LAT, 2 * LAT), 1) // LAT).astype(BF16)

    def half_max(x):
        a = jnp.max(jnp.where(first, x, -jnp.inf), axis=1, keepdims=True)
        b = jnp.max(jnp.where(first, -jnp.inf, x), axis=1, keepdims=True)
        return jnp.where(first, a, b)

    def half_sum(x):
        high = x.astype(BF16)
        low = (x - high.astype(F32)).astype(BF16)
        return dot(high, ones) + dot(low, ones)

    for x in loads[4:]:
        x.wait()

    at = [slice(u * TB, (u + 1) * TB) for u in range(UNROLL)]

    def owner(r):
        return lax.rem(me // 2 + 4 - r % 4, 4) * 2 + lax.rem(me + r // 4, 2)

    def images(r):
        return [blk[owner(r) * UNROLL + u] for u in range(UNROLL)]

    def scores(r):
        img = images(r)
        toks[1][r] = (toks[1][r].astype(F32) * g).astype(BF16)
        for rows, mats, out in ((toks[0], kzt, ss), (toks[1], vzt, pgs)):
            for u in range(0, UNROLL, 2):
                pair = jnp.concatenate([mats[img[u]], mats[img[u + 1]]], axis=1)
                both = dot(rows[r, u * TB : (u + 2) * TB, :], pair)
                out[r, at[u], :] = both[:TB, : 2 * LAT]
                out[r, at[u + 1], :] = both[TB:, 2 * LAT :]

    def weigh(r):
        s, pg = ss[r], pgs[r]
        e = jnp.exp2((s - half_max(s)) * c2)
        prob = e / half_sum(e)
        lows[r] = prob.astype(BF16)
        delta = half_sum(prob * pg)
        sgs[r] = (prob * (pg - delta) * scale).astype(BF16)

    def collect(r):
        img = images(r)
        for u in range(UNROLL):
            lu, su = lows[r, at[u], :], sgs[r, at[u], :]
            made[r, at[u], :] = (dot(lu, vz[img[u]]) * g).astype(BF16)
            made[r, tokens + u * TB : tokens + (u + 1) * TB, :] = dot(su, kz[img[u]]).astype(BF16)
            kt = dot_t(su, toks[0][r, at[u], :])
            vt = dot_t(lu, toks[1][r, at[u], :])
            rows = pl.ds(pl.multiple_of(img[u] * LAT, LAT), LAT)
            acck[rows, :HD] += kt[:LAT, :HD]
            acck[rows, HD:] += kt[LAT:, HD:]
            accv[rows, :HD] += vt[:LAT, :HD]
            accv[rows, HD:] += vt[LAT:, HD:]

    for step in range(10):
        if step < 8:
            scores(step)
        if 1 <= step < 9:
            weigh(step - 1)
        if step >= 2:
            collect(step - 2)
    stores = [pltpu.make_async_copy(made.at[r], oc.at[owner(r)], sems.at[20 + r]) for r in range(8)]
    for x in stores:
        x.start()
    for p in range(PIECES):
        for acc, lo in ((acck, 0), (accv, 2 * HD)):
            x = jnp.concatenate(
                [acc[i * LAT + p * ROWS : i * LAT + (p + 1) * ROWS, :] for i in range(IMAGES)], axis=0
            )
            ki[p * span : (p + 1) * span, lo : lo + 2 * HD] = x.astype(BF16)
    for near, away, rows in ((a0, a1, w_own), (b0, b1, w_other)):
        n = 4 * span
        total = dot_t(near[...].reshape(n, half), ki[:n, :]) + dot_t(away[...].reshape(n, half), ki[n:, :])
        gs[rows, :] = total.astype(BF16)
    n = keep.shape[1]
    for k in range(4):
        give = gs[pl.ds(pl.multiple_of((2 * k + 1 - odd) * n, n), n), :]
        if k == 0:
            lead[0] = give
        else:
            rest[k - 1] = give
        keep[k] = gs[pl.ds(pl.multiple_of((2 * k + odd) * n, n), n), :]
    for x in stores:
        x.wait()


def rotate_kernel(info, q, c, *outs):
    cols = outs[0].shape[2]
    me = info[0]
    for d in range(4):
        for j in range(2):
            to = lax.rem(me // 2 + d, 4) * 2 + lax.rem(me + j, 2)
            off = pl.multiple_of(to * cols, cols)
            outs[d][j] = q[:, pl.ds(off, cols)]
            outs[4 + j][d] = c[:, pl.ds(off, cols)]


def spread_kernel(y, a, b):
    cols, t = y.shape[3], pl.program_id(0)
    rows = pl.ds(pl.multiple_of(t * a.shape[0], a.shape[0]), a.shape[0])
    for r in range(8):
        a[:, r * cols : (r + 1) * cols] = y[r, 0, rows, :]
        b[:, r * cols : (r + 1) * cols] = y[r, 1, rows, :]


def swap(x, axes, pairs):
    return lax.ppermute(x, axes, pairs)


def exchange(x, axes, **kw):
    return lax.all_to_all(x, axes, split_axis=0, concat_axis=0, tiled=True, **kw)


def body(query, latents, image_slot, block_image, key_weight, value_weight, gate, cotangent):
    seq_i, mp_i, dp_i = lax.axis_index("seq"), lax.axis_index("mp"), lax.axis_index("dp")
    tokens, width = query.shape[1], query.shape[2]
    kv = latents.shape[3]
    n_seq = 8
    cols = width // n_seq
    slots = latents.shape[1]
    half = kv // 2
    shape = jax.ShapeDtypeStruct
    info = jnp.stack([seq_i, mp_i, dp_i // 2 % 2]).astype(jnp.int32)
    cut = latents[0].reshape(slots, PIECES, ROWS, 2, half).transpose(1, 3, 0, 2, 4)
    got = exchange(cut.reshape(16, slots * ROWS, half), ("seq", "mp"))

    def along_x(x, d):
        return swap(x, "seq", [(i * 2 + k, (i + d) % 4 * 2 + k) for i in range(4) for k in range(2)])

    def across_y(x):
        return swap(x, "mp", [(0, 1), (1, 0)])

    def sibling(x):
        return swap(x, "seq", [(j, j ^ 1) for j in range(8)])

    turned = pl.pallas_call(
        rotate_kernel,
        out_shape=[shape((2, tokens, cols), BF16)] * 4 + [shape((4, tokens, cols), BF16)] * 2,
        in_specs=[SMEM, VMEM, VMEM],
        out_specs=[VMEM] * 6,
        name="rotate",
    )(info, query[0], cotangent[0])
    q_in = [turned[0], along_x(turned[1], 1), None, along_x(turned[3], 3)]
    from_sib = sibling(turned[5])
    c_out = [jnp.stack([turned[4][d], from_sib[d]]) for d in range(4)]
    got, q_in[1], q_in[3], c_out = lax.optimization_barrier((got, q_in[1], q_in[3], c_out))
    mine = jnp.take(got.reshape(16 * slots, ROWS, half), image_slot[0], axis=0)
    mine, q_far = lax.optimization_barrier((mine.reshape(IMAGES * ROWS, half), turned[2]))
    moved = [along_x(mine, d) for d in (1, -1, 2)]
    q_in[2] = along_x(q_far, 2)
    first = across_y(mine)
    moved, first, c_out = lax.optimization_barrier((moved, first, c_out))
    c_in = [c_out[0]] + [along_x(c_out[d], d) for d in range(1, 4)]
    own, other = [mine] + moved, [first] + [across_y(x) for x in moved]
    q_give = jnp.stack([x[1] for x in q_in])
    q_give, c_in[1:], other[1:] = lax.optimization_barrier((q_give, c_in[1:], other[1:]))
    q_sib = sibling(q_give)
    a0, b0 = jnp.stack(own), jnp.stack(other)
    a1, b1 = sibling(a0), sibling(b0)
    wk, wv = key_weight[:, 0, :], value_weight[:, 0, :]
    n_rows = IMAGES * LAT
    gain = jnp.repeat(jnp.tanh(lax.dynamic_slice_in_dim(gate, seq_i * 2, 2)), HD)[None, :]
    rows = kv // 16
    some = [shape((n, 2 * rows, 4 * HD), BF16) for n in (1, 3, 4)]
    zs, zt = (IMAGES, 2 * LAT, 2 * HD), (IMAGES, 2 * HD, 2 * LAT)
    oc, lead, rest, keep = pl.pallas_call(
        fused_kernel,
        out_shape=(shape((n_seq, 2 * tokens, cols), BF16), *some),
        in_specs=[SMEM, SMEM] + [VMEM] * 3 + [ANY] * 13,
        out_specs=(ANY, VMEM, VMEM, VMEM),
        scratch_shapes=[pltpu.VMEM(x, BF16) for x in (zs, zs, zt, zt)]
        + [pltpu.VMEM((n_rows, 2 * HD), F32)] * 2
        + [pltpu.VMEM((n_rows, 4 * HD), BF16), pltpu.VMEM((kv, 4 * HD), BF16)]
        + [pltpu.VMEM(a0.shape, BF16)] * 4
        + [pltpu.VMEM((n_seq, tokens, cols), BF16)] * 2
        + [pltpu.VMEM((n_seq, 2 * tokens, cols), BF16), pltpu.SemaphoreType.DMA((28,))]
        + [pltpu.VMEM((n_seq, tokens, 2 * LAT), x) for x in (F32, F32, BF16, BF16)],
        compiler_params=pltpu.CompilerParams(vmem_limit_bytes=60 * 2**20),
        cost_estimate=pl.CostEstimate(
            flops=2**33, bytes_accessed=16 * 2**20, transcendentals=2**19
        ),
        name="fused",
    )(info, block_image[0], gain, wk, wv, a0, b0, a1, b1, *q_in, q_sib, *c_in)

    z_i, h_i = dp_i // 2, dp_i % 2
    pairs = []
    for z in range(8):
        for h in range(2):
            for s in range(8):
                if s % 2 == 0:
                    to = z ^ 1
                else:
                    to = (z + 1) % 8 if z % 2 else (z - 1) % 8
                pairs.append(((z * 2 + h) * 8 + s, (to * 2 + h) * 8 + s))

    def pick(x, i, axis):
        return lax.dynamic_index_in_dim(x, i, axis, keepdims=False)

    def join(x, y):
        return (x.astype(F32) + y.astype(F32)).astype(BF16)

    lead = swap(lead, ("dp", "seq"), pairs)
    rest = swap(rest, ("dp", "seq"), pairs)
    lead, oc = lax.optimization_barrier((lead, oc))
    flat_out = shape((tokens, width), BF16)
    attended, query_grad = pl.pallas_call(
        spread_kernel,
        grid=(tokens // 64,),
        out_shape=(flat_out, flat_out),
        in_specs=[VMEM],
        out_specs=[pl.BlockSpec((64, width), lambda t: (t, 0))] * 2,
        name="spread",
    )(exchange(oc, "seq").reshape(n_seq, 2, tokens, cols))

    part = join(keep, jnp.concatenate([lead, rest], axis=0)).reshape(4, 2, rows, 4 * HD)
    part = join(pick(part, h_i, 1), swap(pick(part, 1 - h_i, 1), "dp", [(j, j ^ 1) for j in range(16)]))
    k_i = z_i // 2
    more = []
    for r in range(1, 4):
        perm = [(z * 2 + h, (z + 2 * r) % 8 * 2 + h) for z in range(8) for h in range(2)]
        more.append(swap(pick(part, (k_i + r) % 4, 0), "dp", perm))
    (attended, query_grad), more = lax.optimization_barrier(((attended, query_grad), more))
    total = pick(part, k_i, 0).astype(F32)
    for x in more:
        total = total + x.astype(F32)
    key_grad = total[:, : 2 * HD].reshape(rows, 1, 2 * HD)
    value_grad = total[:, 2 * HD :].reshape(rows, 1, 2 * HD)
    return attended[None], query_grad[None], key_grad, value_grad


def solution(mesh):
    in_specs = (
        P("dp", "seq", "mp"),
        P("dp", ("seq", "mp"), None, None),
        P("dp", None),
        P("dp", None),
        P(None, "mp", "seq"),
        P(None, "mp", "seq"),
        P("mp"),
        P("dp", "seq", "mp"),
    )
    out_specs = (
        P("dp", "seq", "mp"),
        P("dp", "seq", "mp"),
        P("dp", "mp", "seq"),
        P("dp", "mp", "seq"),
    )
    return jax.shard_map(body, mesh=mesh, in_specs=in_specs, out_specs=out_specs, check_vma=False)
```

```python
import math

import jax
import jax.numpy as jnp
from jax import lax
from jax.experimental import pallas as pl
from jax.experimental.pallas import tpu as pltpu
from jax.sharding import PartitionSpec as P

F32, BF16 = jnp.float32, jnp.bfloat16
IMAGES, LAT, HD, TB, UNROLL = 16, 64, 128, 32, 8
PIECES = 8
ROWS = LAT // PIECES
VMEM = pl.BlockSpec(memory_space=pltpu.VMEM)
ANY = pl.BlockSpec(memory_space=pl.ANY)
SMEM = pl.BlockSpec(memory_space=pltpu.SMEM)


def dot(a, b):
    return jnp.dot(a, b, preferred_element_type=F32)


def dot_t(a, b):
    return lax.dot_general(a, b, (((0,), (0,)), ((), ())), preferred_element_type=F32)


def fused_kernel(
    info, blk, gain, wk, wv, *refs
):
    far_parts, far_tok, (oc, send, keep) = refs[:4], refs[4:13], refs[13:16]
    (kz, vz, kzt, vzt, acck, accv, ki, gs), parts, toks, made, sems = refs[16:24], refs[24:28], refs[28:30], *refs[30:32]
    ss, pgs, lows, sgs = refs[32:]
    a0, b0, a1, b1 = parts
    moves = list(zip(far_parts, parts))
    for r in range(8):
        moves.append((far_tok[r].at[0] if r < 4 else far_tok[4].at[r - 4], toks[0].at[r]))
        moves.append((far_tok[5 + r % 4].at[r // 4], toks[1].at[r]))
    loads = [pltpu.make_async_copy(x, y, sems.at[n]) for n, (x, y) in enumerate(moves)]
    for x in loads:
        x.start()
    scale = 1.0 / math.sqrt(HD)
    c2 = scale * math.log2(math.e)
    me, m, odd = info[0], info[1], info[2]
    span = IMAGES * ROWS
    half = a0.shape[2]
    w_own = pl.ds(pl.multiple_of(m * half, half), half)
    w_other = pl.ds(pl.multiple_of((1 - m) * half, half), half)
    for n, (a, b) in enumerate(((a0, b0), (a1, b1))):
        loads[2 * n].wait()
        loads[2 * n + 1].wait()
        x, y = a[...].reshape(4 * span, half), b[...].reshape(4 * span, half)
        rows = slice(n * 4 * span, (n + 1) * 4 * span)
        acck[rows, :] = dot(x, wk[w_own, :]) + dot(y, wk[w_other, :])
        accv[rows, :] = dot(x, wv[w_own, :]) + dot(y, wv[w_other, :])
    zero = jnp.zeros((LAT, HD), F32)
    for i in range(IMAGES):
        for src, plain, turned in ((acck, kz, kzt), (accv, vz, vzt)):
            x = jnp.concatenate(
                [src[p * span + i * ROWS : p * span + (i + 1) * ROWS, :] for p in range(PIECES)], axis=0
            )
            top = jnp.concatenate([x[:, :HD], zero], axis=1)
            low = jnp.concatenate([zero, x[:, HD:]], axis=1)
            both = jnp.concatenate([top, low], axis=0)
            plain[i] = both.astype(BF16)
            turned[i] = both.T.astype(BF16)
    acck[...] = jnp.zeros_like(acck)
    accv[...] = jnp.zeros_like(accv)
    g = gain[...]
    first = lax.broadcasted_iota(jnp.int32, (TB * UNROLL, 2 * LAT), 1) < LAT
    tokens = TB * UNROLL

    ones = lax.broadcasted_iota(jnp.int32, (2 * LAT, 2 * LAT), 0) // LAT
    ones = (ones == lax.broadcasted_iota(jnp.int32, (2 * LAT, 2 * LAT), 1) // LAT).astype(BF16)

    def half_max(x):
        a = jnp.max(jnp.where(first, x, -jnp.inf), axis=1, keepdims=True)
        b = jnp.max(jnp.where(first, -jnp.inf, x), axis=1, keepdims=True)
        return jnp.where(first, a, b)

    def half_sum(x):
        high = x.astype(BF16)
        low = (x - high.astype(F32)).astype(BF16)
        return dot(high, ones) + dot(low, ones)

    for x in loads[4:]:
        x.wait()

    at = [slice(u * TB, (u + 1) * TB) for u in range(UNROLL)]

    def owner(r):
        return lax.rem(me // 2 + 4 - r % 4, 4) * 2 + lax.rem(me + r // 4, 2)

    def images(r):
        return [blk[owner(r) * UNROLL + u] for u in range(UNROLL)]

    def scores(r):
        img = images(r)
        toks[1][r] = (toks[1][r].astype(F32) * g).astype(BF16)
        for rows, mats, out in ((toks[0], kzt, ss), (toks[1], vzt, pgs)):
            for u in range(0, UNROLL, 2):
                pair = jnp.concatenate([mats[img[u]], mats[img[u + 1]]], axis=1)
                both = dot(rows[r, u * TB : (u + 2) * TB, :], pair)
                out[r, at[u], :] = both[:TB, : 2 * LAT]
                out[r, at[u + 1], :] = both[TB:, 2 * LAT :]

    def weigh(r):
        s, pg = ss[r], pgs[r]
        e = jnp.exp2((s - half_max(s)) * c2)
        prob = e / half_sum(e)
        lows[r] = prob.astype(BF16)
        delta = half_sum(prob * pg)
        sgs[r] = (prob * (pg - delta) * scale).astype(BF16)

    def collect(r):
        img = images(r)
        for u in range(UNROLL):
            lu, su = lows[r, at[u], :], sgs[r, at[u], :]
            made[r, at[u], :] = (dot(lu, vz[img[u]]) * g).astype(BF16)
            made[r, tokens + u * TB : tokens + (u + 1) * TB, :] = dot(su, kz[img[u]]).astype(BF16)
            kt = dot_t(su, toks[0][r, at[u], :])
            vt = dot_t(lu, toks[1][r, at[u], :])
            rows = pl.ds(pl.multiple_of(img[u] * LAT, LAT), LAT)
            acck[rows, :HD] += kt[:LAT, :HD]
            acck[rows, HD:] += kt[LAT:, HD:]
            accv[rows, :HD] += vt[:LAT, :HD]
            accv[rows, HD:] += vt[LAT:, HD:]

    for step in range(10):
        if step < 8:
            scores(step)
        if 1 <= step < 9:
            weigh(step - 1)
        if step >= 2:
            collect(step - 2)
    stores = [pltpu.make_async_copy(made.at[r], oc.at[owner(r)], sems.at[20 + r]) for r in range(8)]
    for x in stores:
        x.start()
    for p in range(PIECES):
        for acc, lo in ((acck, 0), (accv, 2 * HD)):
            x = jnp.concatenate(
                [acc[i * LAT + p * ROWS : i * LAT + (p + 1) * ROWS, :] for i in range(IMAGES)], axis=0
            )
            ki[p * span : (p + 1) * span, lo : lo + 2 * HD] = x.astype(BF16)
    for near, away, rows in ((a0, a1, w_own), (b0, b1, w_other)):
        n = 4 * span
        total = dot_t(near[...].reshape(n, half), ki[:n, :]) + dot_t(away[...].reshape(n, half), ki[n:, :])
        gs[rows, :] = total.astype(BF16)
    n = keep.shape[1]
    for k in range(4):
        send[k] = gs[pl.ds(pl.multiple_of((2 * k + 1 - odd) * n, n), n), :]
        keep[k] = gs[pl.ds(pl.multiple_of((2 * k + odd) * n, n), n), :]
    for x in stores:
        x.wait()


def rotate_kernel(info, q, c, *outs):
    cols = outs[0].shape[2]
    me = info[0]
    for d in range(4):
        for j in range(2):
            to = lax.rem(me // 2 + d, 4) * 2 + lax.rem(me + j, 2)
            off = pl.multiple_of(to * cols, cols)
            outs[d][j] = q[:, pl.ds(off, cols)]
            outs[4 + j][d] = c[:, pl.ds(off, cols)]


def spread_kernel(y, a, b):
    cols, t = y.shape[3], pl.program_id(0)
    rows = pl.ds(pl.multiple_of(t * a.shape[0], a.shape[0]), a.shape[0])
    for r in range(8):
        a[:, r * cols : (r + 1) * cols] = y[r, 0, rows, :]
        b[:, r * cols : (r + 1) * cols] = y[r, 1, rows, :]


def total_kernel(a, b, c, d, k, v):
    total = a[...].astype(F32) + b[...].astype(F32) + c[...].astype(F32) + d[...].astype(F32)
    n = total.shape[1] // 2
    k[...] = total[:, None, :n]
    v[...] = total[:, None, n:]


def swap(x, axes, pairs):
    return lax.ppermute(x, axes, pairs)


def exchange(x, axes, **kw):
    return lax.all_to_all(x, axes, split_axis=0, concat_axis=0, tiled=True, **kw)


def body(query, latents, image_slot, block_image, key_weight, value_weight, gate, cotangent):
    seq_i, mp_i, dp_i = lax.axis_index("seq"), lax.axis_index("mp"), lax.axis_index("dp")
    tokens, width = query.shape[1], query.shape[2]
    kv = latents.shape[3]
    n_seq = 8
    cols = width // n_seq
    slots = latents.shape[1]
    half = kv // 2
    shape = jax.ShapeDtypeStruct
    info = jnp.stack([seq_i, mp_i, dp_i // 2 % 2]).astype(jnp.int32)
    cut = latents[0].reshape(slots, PIECES, ROWS, 2, half).transpose(1, 3, 0, 2, 4)
    got = exchange(cut.reshape(16, slots * ROWS, half), ("seq", "mp"))

    def along_x(x, d):
        return swap(x, "seq", [(i * 2 + k, (i + d) % 4 * 2 + k) for i in range(4) for k in range(2)])

    def across_y(x):
        return swap(x, "mp", [(0, 1), (1, 0)])

    def sibling(x):
        return swap(x, "seq", [(j, j ^ 1) for j in range(8)])

    turned = pl.pallas_call(
        rotate_kernel,
        out_shape=[shape((2, tokens, cols), BF16)] * 4 + [shape((4, tokens, cols), BF16)] * 2,
        in_specs=[SMEM, VMEM, VMEM],
        out_specs=[VMEM] * 6,
        name="rotate",
    )(info, query[0], cotangent[0])
    q_in = [turned[0], along_x(turned[1], 1), None, along_x(turned[3], 3)]
    from_sib = sibling(turned[5])
    c_out = [jnp.stack([turned[4][d], from_sib[d]]) for d in range(4)]
    got, q_in[1], q_in[3], c_out = lax.optimization_barrier((got, q_in[1], q_in[3], c_out))
    mine = jnp.take(got.reshape(16 * slots, ROWS, half), image_slot[0], axis=0)
    mine, q_far = lax.optimization_barrier((mine.reshape(IMAGES * ROWS, half), turned[2]))
    moved = [along_x(mine, d) for d in (1, -1, 2)]
    q_in[2] = along_x(q_far, 2)
    first = across_y(mine)
    moved, first, c_out = lax.optimization_barrier((moved, first, c_out))
    c_in = [c_out[0]] + [along_x(c_out[d], d) for d in range(1, 4)]
    own, other = [mine] + moved, [first] + [across_y(x) for x in moved]
    q_give = jnp.stack([x[1] for x in q_in])
    q_give, c_in[1:], other[1:] = lax.optimization_barrier((q_give, c_in[1:], other[1:]))
    q_sib = sibling(q_give)
    a0, b0 = jnp.stack(own), jnp.stack(other)
    a1, b1 = sibling(a0), sibling(b0)
    wk, wv = key_weight[:, 0, :], value_weight[:, 0, :]
    n_rows = IMAGES * LAT
    gain = jnp.repeat(jnp.tanh(lax.dynamic_slice_in_dim(gate, seq_i * 2, 2)), HD)[None, :]
    rows = kv // 16
    some = [shape((4, 2 * rows, 4 * HD), BF16)] * 2
    zs, zt = (IMAGES, 2 * LAT, 2 * HD), (IMAGES, 2 * HD, 2 * LAT)
    oc, send, keep = pl.pallas_call(
        fused_kernel,
        out_shape=(shape((n_seq, 2 * tokens, cols), BF16), *some),
        in_specs=[SMEM, SMEM] + [VMEM] * 3 + [ANY] * 13,
        out_specs=(ANY, VMEM, VMEM),
        scratch_shapes=[pltpu.VMEM(x, BF16) for x in (zs, zs, zt, zt)]
        + [pltpu.VMEM((n_rows, 2 * HD), F32)] * 2
        + [pltpu.VMEM((n_rows, 4 * HD), BF16), pltpu.VMEM((kv, 4 * HD), BF16)]
        + [pltpu.VMEM(a0.shape, BF16)] * 4
        + [pltpu.VMEM((n_seq, tokens, cols), BF16)] * 2
        + [pltpu.VMEM((n_seq, 2 * tokens, cols), BF16), pltpu.SemaphoreType.DMA((28,))]
        + [pltpu.VMEM((n_seq, tokens, 2 * LAT), x) for x in (F32, F32, BF16, BF16)],
        compiler_params=pltpu.CompilerParams(vmem_limit_bytes=60 * 2**20),
        cost_estimate=pl.CostEstimate(
            flops=2**33, bytes_accessed=16 * 2**20, transcendentals=2**19
        ),
        name="fused",
    )(info, block_image[0], gain, wk, wv, a0, b0, a1, b1, *q_in, q_sib, *c_in)

    z_i, h_i = dp_i // 2, dp_i % 2
    pairs = []
    for z in range(8):
        for h in range(2):
            for s in range(8):
                if s % 2 == 0:
                    to = z ^ 1
                else:
                    to = (z + 1) % 8 if z % 2 else (z - 1) % 8
                pairs.append(((z * 2 + h) * 8 + s, (to * 2 + h) * 8 + s))

    def pick(x, i, axis):
        return lax.dynamic_index_in_dim(x, i, axis, keepdims=False)

    def join(x, y):
        return (x.astype(F32) + y.astype(F32)).astype(BF16)

    came = swap(send, ("dp", "seq"), pairs).reshape(4, 2, rows, 4 * HD)
    keep = keep.reshape(4, 2, rows, 4 * HD)
    flat_out = shape((tokens, width), BF16)
    attended, query_grad = pl.pallas_call(
        spread_kernel,
        grid=(tokens // 64,),
        out_shape=(flat_out, flat_out),
        in_specs=[VMEM],
        out_specs=[pl.BlockSpec((64, width), lambda t: (t, 0))] * 2,
        name="spread",
    )(exchange(oc, "seq").reshape(n_seq, 2, tokens, cols))

    give = join(pick(keep, 1 - h_i, 1), pick(came, 1 - h_i, 1))
    back = swap(give, "dp", [(j, j ^ 1) for j in range(16)])
    part = join(join(pick(keep, h_i, 1), pick(came, h_i, 1)), back)
    k_i = z_i // 2
    more = []
    for r in range(1, 4):
        perm = [(z * 2 + h, (z + 2 * r) % 8 * 2 + h) for z in range(8) for h in range(2)]
        more.append(swap(pick(part, (k_i + r) % 4, 0), "dp", perm))
    (attended, query_grad), more = lax.optimization_barrier(((attended, query_grad), more))
    one = shape((rows, 1, 2 * HD), F32)
    key_grad, value_grad = pl.pallas_call(
        total_kernel,
        out_shape=(one, one),
        in_specs=[VMEM] * 4,
        out_specs=(VMEM, VMEM),
        name="total",
    )(pick(part, k_i, 0), *more)
    return attended[None], query_grad[None], key_grad, value_grad


def solution(mesh):
    in_specs = (
        P("dp", "seq", "mp"),
        P("dp", ("seq", "mp"), None, None),
        P("dp", None),
        P("dp", None),
        P(None, "mp", "seq"),
        P(None, "mp", "seq"),
        P("mp"),
        P("dp", "seq", "mp"),
    )
    out_specs = (
        P("dp", "seq", "mp"),
        P("dp", "seq", "mp"),
        P("dp", "mp", "seq"),
        P("dp", "mp", "seq"),
    )
    return jax.shard_map(body, mesh=mesh, in_specs=in_specs, out_specs=out_specs, check_vma=False)
```

```python
import math

import jax
import jax.numpy as jnp
from jax import lax
from jax.experimental import pallas as pl
from jax.experimental.pallas import tpu as pltpu
from jax.sharding import PartitionSpec as P

F32, BF16 = jnp.float32, jnp.bfloat16
IMAGES, LAT, HD, TB, UNROLL = 16, 64, 128, 32, 8
PIECES = 8
ROWS = LAT // PIECES
VMEM = pl.BlockSpec(memory_space=pltpu.VMEM)
ANY = pl.BlockSpec(memory_space=pl.ANY)
SMEM = pl.BlockSpec(memory_space=pltpu.SMEM)


def dot(a, b):
    return jnp.dot(a, b, preferred_element_type=F32)


def dot_t(a, b):
    return lax.dot_general(a, b, (((0,), (0,)), ((), ())), preferred_element_type=F32)


def fused_kernel(
    info, blk, gain, wk, wv, *refs
):
    far_parts, far_tok, (oc, send, keep) = refs[:4], refs[4:13], refs[13:16]
    (kz, vz, kzt, vzt, acck, accv, ki, gs), parts, toks, made, sems = refs[16:24], refs[24:28], refs[28:30], *refs[30:32]
    ss, pgs, lows, sgs = refs[32:]
    a0, b0, a1, b1 = parts
    moves = list(zip(far_parts, parts))
    for r in range(8):
        moves.append((far_tok[r].at[0] if r < 4 else far_tok[4].at[r - 4], toks[0].at[r]))
        moves.append((far_tok[5 + r % 4].at[r // 4], toks[1].at[r]))
    loads = [pltpu.make_async_copy(x, y, sems.at[n]) for n, (x, y) in enumerate(moves)]
    for x in loads:
        x.start()
    scale = 1.0 / math.sqrt(HD)
    c2 = scale * math.log2(math.e)
    me, m, odd = info[0], info[1], info[2]
    span = IMAGES * ROWS
    half = a0.shape[2]
    w_own = pl.ds(pl.multiple_of(m * half, half), half)
    w_other = pl.ds(pl.multiple_of((1 - m) * half, half), half)
    for n, (a, b) in enumerate(((a0, b0), (a1, b1))):
        loads[2 * n].wait()
        loads[2 * n + 1].wait()
        x, y = a[...].reshape(4 * span, half), b[...].reshape(4 * span, half)
        rows = slice(n * 4 * span, (n + 1) * 4 * span)
        acck[rows, :] = dot(x, wk[w_own, :]) + dot(y, wk[w_other, :])
        accv[rows, :] = dot(x, wv[w_own, :]) + dot(y, wv[w_other, :])
    zero = jnp.zeros((LAT, HD), F32)
    for i in range(IMAGES):
        for src, plain, turned in ((acck, kz, kzt), (accv, vz, vzt)):
            x = jnp.concatenate(
                [src[p * span + i * ROWS : p * span + (i + 1) * ROWS, :] for p in range(PIECES)], axis=0
            )
            top = jnp.concatenate([x[:, :HD], zero], axis=1)
            low = jnp.concatenate([zero, x[:, HD:]], axis=1)
            both = jnp.concatenate([top, low], axis=0)
            plain[i] = both.astype(BF16)
            turned[i] = both.T.astype(BF16)
    acck[...] = jnp.zeros_like(acck)
    accv[...] = jnp.zeros_like(accv)
    g = gain[...]
    first = lax.broadcasted_iota(jnp.int32, (TB * UNROLL, 2 * LAT), 1) < LAT
    tokens = TB * UNROLL

    ones = lax.broadcasted_iota(jnp.int32, (2 * LAT, 2 * LAT), 0) // LAT
    ones = (ones == lax.broadcasted_iota(jnp.int32, (2 * LAT, 2 * LAT), 1) // LAT).astype(BF16)

    def half_max(x):
        a = jnp.max(jnp.where(first, x, -jnp.inf), axis=1, keepdims=True)
        b = jnp.max(jnp.where(first, -jnp.inf, x), axis=1, keepdims=True)
        return jnp.where(first, a, b)

    def half_sum(x):
        high = x.astype(BF16)
        low = (x - high.astype(F32)).astype(BF16)
        return dot(high, ones) + dot(low, ones)

    for x in loads[4:]:
        x.wait()

    at = [slice(u * TB, (u + 1) * TB) for u in range(UNROLL)]

    def owner(r):
        return lax.rem(me // 2 + 4 - r % 4, 4) * 2 + lax.rem(me + r // 4, 2)

    def images(r):
        return [blk[owner(r) * UNROLL + u] for u in range(UNROLL)]

    def scores(r):
        img = images(r)
        toks[1][r] = (toks[1][r].astype(F32) * g).astype(BF16)
        for rows, mats, out in ((toks[0], kzt, ss), (toks[1], vzt, pgs)):
            for u in range(0, UNROLL, 2):
                pair = jnp.concatenate([mats[img[u]], mats[img[u + 1]]], axis=1)
                both = dot(rows[r, u * TB : (u + 2) * TB, :], pair)
                out[r, at[u], :] = both[:TB, : 2 * LAT]
                out[r, at[u + 1], :] = both[TB:, 2 * LAT :]

    def weigh(r):
        s, pg = ss[r], pgs[r]
        e = jnp.exp2((s - half_max(s)) * c2)
        prob = e / half_sum(e)
        lows[r] = prob.astype(BF16)
        delta = half_sum(prob * pg)
        sgs[r] = (prob * (pg - delta) * scale).astype(BF16)

    def collect(r):
        img = images(r)
        for u in range(UNROLL):
            lu, su = lows[r, at[u], :], sgs[r, at[u], :]
            made[r, at[u], :] = (dot(lu, vz[img[u]]) * g).astype(BF16)
            made[r, tokens + u * TB : tokens + (u + 1) * TB, :] = dot(su, kz[img[u]]).astype(BF16)
            kt = dot_t(su, toks[0][r, at[u], :])
            vt = dot_t(lu, toks[1][r, at[u], :])
            rows = pl.ds(pl.multiple_of(img[u] * LAT, LAT), LAT)
            acck[rows, :HD] += kt[:LAT, :HD]
            acck[rows, HD:] += kt[LAT:, HD:]
            accv[rows, :HD] += vt[:LAT, :HD]
            accv[rows, HD:] += vt[LAT:, HD:]

    for step in range(10):
        if step < 8:
            scores(step)
        if 1 <= step < 9:
            weigh(step - 1)
        if step >= 2:
            collect(step - 2)
    stores = [pltpu.make_async_copy(made.at[r], oc.at[owner(r)], sems.at[20 + r]) for r in range(8)]
    for x in stores:
        x.start()
    for p in range(PIECES):
        for acc, lo in ((acck, 0), (accv, 2 * HD)):
            x = jnp.concatenate(
                [acc[i * LAT + p * ROWS : i * LAT + (p + 1) * ROWS, :] for i in range(IMAGES)], axis=0
            )
            ki[p * span : (p + 1) * span, lo : lo + 2 * HD] = x.astype(BF16)
    for near, away, rows in ((a0, a1, w_own), (b0, b1, w_other)):
        n = 4 * span
        total = dot_t(near[...].reshape(n, half), ki[:n, :]) + dot_t(away[...].reshape(n, half), ki[n:, :])
        gs[rows, :] = total.astype(BF16)
    n = keep.shape[1]
    for k in range(4):
        send[k] = gs[pl.ds(pl.multiple_of((2 * k + 1 - odd) * n, n), n), :]
        keep[k] = gs[pl.ds(pl.multiple_of((2 * k + odd) * n, n), n), :]
    for x in stores:
        x.wait()


def rotate_kernel(info, q, c, *outs):
    cols = outs[0].shape[2]
    me = info[0]
    for d in range(4):
        for j in range(2):
            to = lax.rem(me // 2 + d, 4) * 2 + lax.rem(me + j, 2)
            off = pl.multiple_of(to * cols, cols)
            outs[d][j] = q[:, pl.ds(off, cols)]
            outs[4 + j][d] = c[:, pl.ds(off, cols)]


def spread_kernel(y, a, b):
    cols, t = y.shape[3], pl.program_id(0)
    rows = pl.ds(pl.multiple_of(t * a.shape[0], a.shape[0]), a.shape[0])
    for r in range(8):
        a[:, r * cols : (r + 1) * cols] = y[r, 0, rows, :]
        b[:, r * cols : (r + 1) * cols] = y[r, 1, rows, :]


def total_kernel(a, b, c, d, k, v):
    total = a[...].astype(F32) + b[...].astype(F32) + c[...].astype(F32) + d[...].astype(F32)
    n = total.shape[1] // 2
    k[...] = total[:, None, :n]
    v[...] = total[:, None, n:]


def swap(x, axes, pairs):
    return lax.ppermute(x, axes, pairs)


def exchange(x, axes, **kw):
    return lax.all_to_all(x, axes, split_axis=0, concat_axis=0, tiled=True, **kw)


def body(query, latents, image_slot, block_image, key_weight, value_weight, gate, cotangent):
    seq_i, mp_i, dp_i = lax.axis_index("seq"), lax.axis_index("mp"), lax.axis_index("dp")
    tokens, width = query.shape[1], query.shape[2]
    kv = latents.shape[3]
    n_seq = 8
    cols = width // n_seq
    slots = latents.shape[1]
    half = kv // 2
    shape = jax.ShapeDtypeStruct
    info = jnp.stack([seq_i, mp_i, dp_i // 2 % 2]).astype(jnp.int32)
    cut = latents[0].reshape(slots, PIECES, ROWS, 2, half).transpose(1, 3, 0, 2, 4)
    got = exchange(cut.reshape(16, slots * ROWS, half), ("seq", "mp"))

    def along_x(x, d):
        return swap(x, "seq", [(i * 2 + k, (i + d) % 4 * 2 + k) for i in range(4) for k in range(2)])

    def across_y(x):
        return swap(x, "mp", [(0, 1), (1, 0)])

    def sibling(x):
        return swap(x, "seq", [(j, j ^ 1) for j in range(8)])

    turned = pl.pallas_call(
        rotate_kernel,
        out_shape=[shape((2, tokens, cols), BF16)] * 4 + [shape((4, tokens, cols), BF16)] * 2,
        in_specs=[SMEM, VMEM, VMEM],
        out_specs=[VMEM] * 6,
        name="rotate",
    )(info, query[0], cotangent[0])
    q_in = [turned[0], along_x(turned[1], 1), None, along_x(turned[3], 3)]
    from_sib = sibling(turned[5])
    c_out = [jnp.stack([turned[4][d], from_sib[d]]) for d in range(4)]
    got, q_in[1], q_in[3], c_out = lax.optimization_barrier((got, q_in[1], q_in[3], c_out))
    mine = jnp.take(got.reshape(16 * slots, ROWS, half), image_slot[0], axis=0)
    mine, q_far = lax.optimization_barrier((mine.reshape(IMAGES * ROWS, half), turned[2]))
    moved = [along_x(mine, d) for d in (1, -1, 2)]
    q_in[2] = along_x(q_far, 2)
    first = across_y(mine)
    moved, first, c_out = lax.optimization_barrier((moved, first, c_out))
    c_in = [c_out[0]] + [along_x(c_out[d], d) for d in range(1, 4)]
    own, other = [mine] + moved, [first] + [across_y(x) for x in moved]
    q_give = jnp.stack([x[1] for x in q_in])
    q_give, c_in[1:], other[1:] = lax.optimization_barrier((q_give, c_in[1:], other[1:]))
    q_sib = sibling(q_give)
    a0, b0 = jnp.stack(own), jnp.stack(other)
    a1, b1 = sibling(a0), sibling(b0)
    wk, wv = key_weight[:, 0, :], value_weight[:, 0, :]
    n_rows = IMAGES * LAT
    gain = jnp.repeat(jnp.tanh(lax.dynamic_slice_in_dim(gate, seq_i * 2, 2)), HD)[None, :]
    rows = kv // 16
    some = [shape((4, 2 * rows, 4 * HD), BF16)] * 2
    zs, zt = (IMAGES, 2 * LAT, 2 * HD), (IMAGES, 2 * HD, 2 * LAT)
    oc, send, keep = pl.pallas_call(
        fused_kernel,
        out_shape=(shape((n_seq, 2 * tokens, cols), BF16), *some),
        in_specs=[SMEM, SMEM] + [VMEM] * 3 + [ANY] * 13,
        out_specs=(ANY, VMEM, VMEM),
        scratch_shapes=[pltpu.VMEM(x, BF16) for x in (zs, zs, zt, zt)]
        + [pltpu.VMEM((n_rows, 2 * HD), F32)] * 2
        + [pltpu.VMEM((n_rows, 4 * HD), BF16), pltpu.VMEM((kv, 4 * HD), BF16)]
        + [pltpu.VMEM(a0.shape, BF16)] * 4
        + [pltpu.VMEM((n_seq, tokens, cols), BF16)] * 2
        + [pltpu.VMEM((n_seq, 2 * tokens, cols), BF16), pltpu.SemaphoreType.DMA((28,))]
        + [pltpu.VMEM((n_seq, tokens, 2 * LAT), x) for x in (F32, F32, BF16, BF16)],
        compiler_params=pltpu.CompilerParams(vmem_limit_bytes=60 * 2**20),
        cost_estimate=pl.CostEstimate(
            flops=2**33, bytes_accessed=16 * 2**20, transcendentals=2**19
        ),
        name="fused",
    )(info, block_image[0], gain, wk, wv, a0, b0, a1, b1, *q_in, q_sib, *c_in)

    z_i, h_i = dp_i // 2, dp_i % 2
    pairs = []
    for z in range(8):
        for h in range(2):
            for s in range(8):
                if s % 2 == 0:
                    to = z ^ 1
                else:
                    to = (z + 1) % 8 if z % 2 else (z - 1) % 8
                pairs.append(((z * 2 + h) * 8 + s, (to * 2 + h) * 8 + s))

    def pick(x, i, axis):
        return lax.dynamic_index_in_dim(x, i, axis, keepdims=False)

    def join(x, y):
        return (x.astype(F32) + y.astype(F32)).astype(BF16)

    came = swap(send, ("dp", "seq"), pairs).reshape(4, 2, rows, 4 * HD)
    keep = keep.reshape(4, 2, rows, 4 * HD)
    flat_out = shape((tokens, width), BF16)
    attended, query_grad = pl.pallas_call(
        spread_kernel,
        grid=(tokens // 64,),
        out_shape=(flat_out, flat_out),
        in_specs=[VMEM],
        out_specs=[pl.BlockSpec((64, width), lambda t: (t, 0))] * 2,
        name="spread",
    )(exchange(oc, "seq").reshape(n_seq, 2, tokens, cols))

    give = join(pick(keep, 1 - h_i, 1), pick(came, 1 - h_i, 1))
    back = swap(give, "dp", [(j, j ^ 1) for j in range(16)])
    part = join(join(pick(keep, h_i, 1), pick(came, h_i, 1)), back)
    k_i = z_i // 2
    more = []
    for r in range(1, 4):
        perm = [(z * 2 + h, (z + 2 * r) % 8 * 2 + h) for z in range(8) for h in range(2)]
        more.append(swap(pick(part, (k_i + r) % 4, 0), "dp", perm))
    one = shape((rows, 1, 2 * HD), F32)
    key_grad, value_grad = pl.pallas_call(
        total_kernel,
        out_shape=(one, one),
        in_specs=[VMEM] * 4,
        out_specs=(VMEM, VMEM),
        name="total",
    )(pick(part, k_i, 0), *more)
    return attended[None], query_grad[None], key_grad, value_grad


def solution(mesh):
    in_specs = (
        P("dp", "seq", "mp"),
        P("dp", ("seq", "mp"), None, None),
        P("dp", None),
        P("dp", None),
        P(None, "mp", "seq"),
        P(None, "mp", "seq"),
        P("mp"),
        P("dp", "seq", "mp"),
    )
    out_specs = (
        P("dp", "seq", "mp"),
        P("dp", "seq", "mp"),
        P("dp", "mp", "seq"),
        P("dp", "mp", "seq"),
    )
    return jax.shard_map(body, mesh=mesh, in_specs=in_specs, out_specs=out_specs, check_vma=False)
```

```python
import math

import jax
import jax.numpy as jnp
from jax import lax
from jax.experimental import pallas as pl
from jax.experimental.pallas import tpu as pltpu
from jax.sharding import PartitionSpec as P

F32, BF16 = jnp.float32, jnp.bfloat16
IMAGES, LAT, HD, TB, UNROLL = 16, 64, 128, 32, 8
PIECES = 8
ROWS = LAT // PIECES
VMEM = pl.BlockSpec(memory_space=pltpu.VMEM)
ANY = pl.BlockSpec(memory_space=pl.ANY)
SMEM = pl.BlockSpec(memory_space=pltpu.SMEM)


def dot(a, b):
    return jnp.dot(a, b, preferred_element_type=F32)


def dot_t(a, b):
    return lax.dot_general(a, b, (((0,), (0,)), ((), ())), preferred_element_type=F32)


def fused_kernel(
    info, blk, gain, wk, wv, *refs
):
    far_parts, far_tok, (oc, send, keep) = refs[:4], refs[4:13], refs[13:16]
    (kz, vz, kzt, vzt, acck, accv, ki, gs), parts, toks, made, sems = refs[16:24], refs[24:28], refs[28:30], *refs[30:32]
    ss, pgs, lows, sgs = refs[32:]
    a0, b0, a1, b1 = parts
    moves = list(zip(far_parts, parts))
    for r in range(8):
        moves.append((far_tok[r].at[0] if r < 4 else far_tok[4].at[r - 4], toks[0].at[r]))
        moves.append((far_tok[5 + r % 4].at[r // 4], toks[1].at[r]))
    loads = [pltpu.make_async_copy(x, y, sems.at[n]) for n, (x, y) in enumerate(moves)]
    for x in loads:
        x.start()
    scale = 1.0 / math.sqrt(HD)
    c2 = scale * math.log2(math.e)
    me, m, odd = info[0], info[1], info[2]
    span = IMAGES * ROWS
    half = a0.shape[2]
    w_own = pl.ds(pl.multiple_of(m * half, half), half)
    w_other = pl.ds(pl.multiple_of((1 - m) * half, half), half)
    for n, (a, b) in enumerate(((a0, b0), (a1, b1))):
        loads[2 * n].wait()
        loads[2 * n + 1].wait()
        x, y = a[...].reshape(4 * span, half), b[...].reshape(4 * span, half)
        rows = slice(n * 4 * span, (n + 1) * 4 * span)
        acck[rows, :] = dot(x, wk[w_own, :]) + dot(y, wk[w_other, :])
        accv[rows, :] = dot(x, wv[w_own, :]) + dot(y, wv[w_other, :])
    zero = jnp.zeros((LAT, HD), F32)
    for i in range(IMAGES):
        for src, plain, turned in ((acck, kz, kzt), (accv, vz, vzt)):
            x = jnp.concatenate(
                [src[p * span + i * ROWS : p * span + (i + 1) * ROWS, :] for p in range(PIECES)], axis=0
            )
            top = jnp.concatenate([x[:, :HD], zero], axis=1)
            low = jnp.concatenate([zero, x[:, HD:]], axis=1)
            both = jnp.concatenate([top, low], axis=0)
            plain[i] = both.astype(BF16)
            turned[i] = both.T.astype(BF16)
    acck[...] = jnp.zeros_like(acck)
    accv[...] = jnp.zeros_like(accv)
    g = gain[...]
    first = lax.broadcasted_iota(jnp.int32, (TB * UNROLL, 2 * LAT), 1) < LAT
    tokens = TB * UNROLL

    ones = lax.broadcasted_iota(jnp.int32, (2 * LAT, 2 * LAT), 0) // LAT
    ones = (ones == lax.broadcasted_iota(jnp.int32, (2 * LAT, 2 * LAT), 1) // LAT).astype(BF16)

    def half_max(x):
        a = jnp.max(jnp.where(first, x, -jnp.inf), axis=1, keepdims=True)
        b = jnp.max(jnp.where(first, -jnp.inf, x), axis=1, keepdims=True)
        return jnp.where(first, a, b)

    def half_sum(x):
        high = x.astype(BF16)
        low = (x - high.astype(F32)).astype(BF16)
        return dot(high, ones) + dot(low, ones)

    for x in loads[4:]:
        x.wait()

    at = [slice(u * TB, (u + 1) * TB) for u in range(UNROLL)]

    def owner(r):
        return lax.rem(me // 2 + 4 - r % 4, 4) * 2 + lax.rem(me + r // 4, 2)

    def images(r):
        return [blk[owner(r) * UNROLL + u] for u in range(UNROLL)]

    def scores(r):
        img = images(r)
        toks[1][r] = (toks[1][r].astype(F32) * g).astype(BF16)
        for rows, mats, out in ((toks[0], kzt, ss), (toks[1], vzt, pgs)):
            for u in range(0, UNROLL, 2):
                pair = jnp.concatenate([mats[img[u]], mats[img[u + 1]]], axis=1)
                both = dot(rows[r, u * TB : (u + 2) * TB, :], pair)
                out[r, at[u], :] = both[:TB, : 2 * LAT]
                out[r, at[u + 1], :] = both[TB:, 2 * LAT :]

    def weigh(r):
        s, pg = ss[r], pgs[r]
        e = jnp.exp2((s - half_max(s)) * c2)
        prob = e / half_sum(e)
        lows[r] = prob.astype(BF16)
        delta = half_sum(prob * pg)
        sgs[r] = (prob * (pg - delta) * scale).astype(BF16)

    def collect(r):
        img = images(r)
        for u in range(UNROLL):
            lu, su = lows[r, at[u], :], sgs[r, at[u], :]
            made[r, at[u], :] = (dot(lu, vz[img[u]]) * g).astype(BF16)
            made[r, tokens + u * TB : tokens + (u + 1) * TB, :] = dot(su, kz[img[u]]).astype(BF16)
            kt = dot_t(su, toks[0][r, at[u], :])
            vt = dot_t(lu, toks[1][r, at[u], :])
            rows = pl.ds(pl.multiple_of(img[u] * LAT, LAT), LAT)
            acck[rows, :HD] += kt[:LAT, :HD]
            acck[rows, HD:] += kt[LAT:, HD:]
            accv[rows, :HD] += vt[:LAT, :HD]
            accv[rows, HD:] += vt[LAT:, HD:]

    for step in range(10):
        if step < 8:
            scores(step)
        if 1 <= step < 9:
            weigh(step - 1)
        if step >= 2:
            collect(step - 2)
    stores = [pltpu.make_async_copy(made.at[r], oc.at[owner(r)], sems.at[20 + r]) for r in range(8)]
    for x in stores:
        x.start()
    for p in range(PIECES):
        for acc, lo in ((acck, 0), (accv, 2 * HD)):
            x = jnp.concatenate(
                [acc[i * LAT + p * ROWS : i * LAT + (p + 1) * ROWS, :] for i in range(IMAGES)], axis=0
            )
            ki[p * span : (p + 1) * span, lo : lo + 2 * HD] = x.astype(BF16)
    for near, away, rows in ((a0, a1, w_own), (b0, b1, w_other)):
        n = 4 * span
        total = dot_t(near[...].reshape(n, half), ki[:n, :]) + dot_t(away[...].reshape(n, half), ki[n:, :])
        gs[rows, :] = total.astype(BF16)
    n = keep.shape[1]
    for k in range(4):
        send[k] = gs[pl.ds(pl.multiple_of((2 * k + 1 - odd) * n, n), n), :]
        keep[k] = gs[pl.ds(pl.multiple_of((2 * k + odd) * n, n), n), :]
    for x in stores:
        x.wait()


def rotate_kernel(info, q, c, *outs):
    cols = outs[0].shape[2]
    me = info[0]
    for d in range(4):
        for j in range(2):
            to = lax.rem(me // 2 + d, 4) * 2 + lax.rem(me + j, 2)
            off = pl.multiple_of(to * cols, cols)
            outs[d][j] = q[:, pl.ds(off, cols)]
            outs[4 + j][d] = c[:, pl.ds(off, cols)]


def spread_kernel(y, a, b):
    cols, t = y.shape[3], pl.program_id(0)
    rows = pl.ds(pl.multiple_of(t * a.shape[0], a.shape[0]), a.shape[0])
    for r in range(8):
        a[:, r * cols : (r + 1) * cols] = y[r, 0, rows, :]
        b[:, r * cols : (r + 1) * cols] = y[r, 1, rows, :]


def total_kernel(a, b, c, d, k, v):
    total = a[...].astype(F32) + b[...].astype(F32) + c[...].astype(F32) + d[...].astype(F32)
    n = total.shape[1] // 2
    k[...] = total[:, None, :n]
    v[...] = total[:, None, n:]


def swap(x, axes, pairs):
    return lax.ppermute(x, axes, pairs)


def exchange(x, axes, **kw):
    return lax.all_to_all(x, axes, split_axis=0, concat_axis=0, tiled=True, **kw)


def body(query, latents, image_slot, block_image, key_weight, value_weight, gate, cotangent):
    seq_i, mp_i, dp_i = lax.axis_index("seq"), lax.axis_index("mp"), lax.axis_index("dp")
    tokens, width = query.shape[1], query.shape[2]
    kv = latents.shape[3]
    n_seq = 8
    cols = width // n_seq
    slots = latents.shape[1]
    half = kv // 2
    shape = jax.ShapeDtypeStruct
    info = jnp.stack([seq_i, mp_i, dp_i // 2 % 2]).astype(jnp.int32)
    cut = latents[0].reshape(slots, PIECES, ROWS, 2, half).transpose(1, 3, 0, 2, 4)
    got = exchange(cut.reshape(16, slots * ROWS, half), ("seq", "mp"))

    def along_x(x, d):
        return swap(x, "seq", [(i * 2 + k, (i + d) % 4 * 2 + k) for i in range(4) for k in range(2)])

    def across_y(x):
        return swap(x, "mp", [(0, 1), (1, 0)])

    def sibling(x):
        return swap(x, "seq", [(j, j ^ 1) for j in range(8)])

    turned = pl.pallas_call(
        rotate_kernel,
        out_shape=[shape((2, tokens, cols), BF16)] * 4 + [shape((4, tokens, cols), BF16)] * 2,
        in_specs=[SMEM, VMEM, VMEM],
        out_specs=[VMEM] * 6,
        compiler_params=pltpu.CompilerParams(vmem_limit_bytes=8 * 2**20),
        name="rotate",
    )(info, query[0], cotangent[0])
    q_in = [turned[0], along_x(turned[1], 1), None, along_x(turned[3], 3)]
    from_sib = sibling(turned[5])
    c_out = [jnp.stack([turned[4][d], from_sib[d]]) for d in range(4)]
    got, q_in[1], q_in[3], c_out = lax.optimization_barrier((got, q_in[1], q_in[3], c_out))
    mine = jnp.take(got.reshape(16 * slots, ROWS, half), image_slot[0], axis=0)
    mine, q_far = lax.optimization_barrier((mine.reshape(IMAGES * ROWS, half), turned[2]))
    moved = [along_x(mine, d) for d in (1, -1, 2)]
    q_in[2] = along_x(q_far, 2)
    first = across_y(mine)
    moved, first, c_out = lax.optimization_barrier((moved, first, c_out))
    c_in = [c_out[0]] + [along_x(c_out[d], d) for d in range(1, 4)]
    own, other = [mine] + moved, [first] + [across_y(x) for x in moved]
    q_give = jnp.stack([x[1] for x in q_in])
    q_give, c_in[1:], other[1:] = lax.optimization_barrier((q_give, c_in[1:], other[1:]))
    q_sib = sibling(q_give)
    a0, b0 = jnp.stack(own), jnp.stack(other)
    a1, b1 = sibling(a0), sibling(b0)
    wk, wv = key_weight[:, 0, :], value_weight[:, 0, :]
    n_rows = IMAGES * LAT
    gain = jnp.repeat(jnp.tanh(lax.dynamic_slice_in_dim(gate, seq_i * 2, 2)), HD)[None, :]
    rows = kv // 16
    some = [shape((4, 2 * rows, 4 * HD), BF16)] * 2
    zs, zt = (IMAGES, 2 * LAT, 2 * HD), (IMAGES, 2 * HD, 2 * LAT)
    oc, send, keep = pl.pallas_call(
        fused_kernel,
        out_shape=(shape((n_seq, 2 * tokens, cols), BF16), *some),
        in_specs=[SMEM, SMEM] + [VMEM] * 3 + [ANY] * 13,
        out_specs=(ANY, VMEM, VMEM),
        scratch_shapes=[pltpu.VMEM(x, BF16) for x in (zs, zs, zt, zt)]
        + [pltpu.VMEM((n_rows, 2 * HD), F32)] * 2
        + [pltpu.VMEM((n_rows, 4 * HD), BF16), pltpu.VMEM((kv, 4 * HD), BF16)]
        + [pltpu.VMEM(a0.shape, BF16)] * 4
        + [pltpu.VMEM((n_seq, tokens, cols), BF16)] * 2
        + [pltpu.VMEM((n_seq, 2 * tokens, cols), BF16), pltpu.SemaphoreType.DMA((28,))]
        + [pltpu.VMEM((n_seq, tokens, 2 * LAT), x) for x in (F32, F32, BF16, BF16)],
        compiler_params=pltpu.CompilerParams(vmem_limit_bytes=60 * 2**20),
        cost_estimate=pl.CostEstimate(
            flops=2**33, bytes_accessed=16 * 2**20, transcendentals=2**19
        ),
        name="fused",
    )(info, block_image[0], gain, wk, wv, a0, b0, a1, b1, *q_in, q_sib, *c_in)

    z_i, h_i = dp_i // 2, dp_i % 2
    pairs = []
    for z in range(8):
        for h in range(2):
            for s in range(8):
                if s % 2 == 0:
                    to = z ^ 1
                else:
                    to = (z + 1) % 8 if z % 2 else (z - 1) % 8
                pairs.append(((z * 2 + h) * 8 + s, (to * 2 + h) * 8 + s))

    def pick(x, i, axis):
        return lax.dynamic_index_in_dim(x, i, axis, keepdims=False)

    def join(x, y):
        return (x.astype(F32) + y.astype(F32)).astype(BF16)

    came = swap(send, ("dp", "seq"), pairs).reshape(4, 2, rows, 4 * HD)
    keep = keep.reshape(4, 2, rows, 4 * HD)
    flat_out = shape((tokens, width), BF16)
    attended, query_grad = pl.pallas_call(
        spread_kernel,
        grid=(tokens // 64,),
        out_shape=(flat_out, flat_out),
        in_specs=[VMEM],
        out_specs=[pl.BlockSpec((64, width), lambda t: (t, 0))] * 2,
        compiler_params=pltpu.CompilerParams(vmem_limit_bytes=6 * 2**20),
        name="spread",
    )(exchange(oc, "seq").reshape(n_seq, 2, tokens, cols))

    give = join(pick(keep, 1 - h_i, 1), pick(came, 1 - h_i, 1))
    back = swap(give, "dp", [(j, j ^ 1) for j in range(16)])
    part = join(join(pick(keep, h_i, 1), pick(came, h_i, 1)), back)
    k_i = z_i // 2
    more = []
    for r in range(1, 4):
        perm = [(z * 2 + h, (z + 2 * r) % 8 * 2 + h) for z in range(8) for h in range(2)]
        more.append(swap(pick(part, (k_i + r) % 4, 0), "dp", perm))
    (attended, query_grad), more = lax.optimization_barrier(((attended, query_grad), more))
    one = shape((rows, 1, 2 * HD), F32)
    key_grad, value_grad = pl.pallas_call(
        total_kernel,
        out_shape=(one, one),
        in_specs=[VMEM] * 4,
        out_specs=(VMEM, VMEM),
        compiler_params=pltpu.CompilerParams(vmem_limit_bytes=4 * 2**20),
        name="total",
    )(pick(part, k_i, 0), *more)
    return attended[None], query_grad[None], key_grad, value_grad


def solution(mesh):
    in_specs = (
        P("dp", "seq", "mp"),
        P("dp", ("seq", "mp"), None, None),
        P("dp", None),
        P("dp", None),
        P(None, "mp", "seq"),
        P(None, "mp", "seq"),
        P("mp"),
        P("dp", "seq", "mp"),
    )
    out_specs = (
        P("dp", "seq", "mp"),
        P("dp", "seq", "mp"),
        P("dp", "mp", "seq"),
        P("dp", "mp", "seq"),
    )
    return jax.shard_map(body, mesh=mesh, in_specs=in_specs, out_specs=out_specs, check_vma=False)
```
